128 devices in a mesh: gx: 8 (over x, core), gy: 16 (over y, z).
Axes of the slice: x: 4, y: 4, z: 4, core: 2. Of those that a mesh axis runs over, the one named last changes fastest.
Arguments:
- part_data: bfloat16 [16, 64, 16, 4, 128], P('gx', 'gy'), may hold values from 0 to 1
- tile_cells: int32 [16, 64, 16, 128], P('gx', 'gy'), may hold values from 0 to 511
- tile_counts: int32 [16, 64, 16], P('gx', 'gy'), may hold values from 32 to 128
- ghost_data: bfloat16 [128, 9, 16, 4, 2048], P(('gx', 'gy')), may hold values from 0 to 1
- halo_refined_cells: int32 [128, 9, 16, 2048], P(('gx', 'gy')), may hold values from 0 to 3822, as said below
- ghost_counts: int32 [128, 9, 16], P(('gx', 'gy')), may hold values from 0 to 2048
- virt_data: bfloat16 [128, 9, 4, 512], P(('gx', 'gy')), may hold values from 0 to 1
- virt_cells: int32 [128, 9, 512], P(('gx', 'gy')), may hold values from 0 to 61311, as said below
- phantom_slot_counts: int32 [128, 9], P(('gx', 'gy')), may hold values from 0 to 512
Outputs:
- base_mass: float32 [128, 512, 128], P('gx', 'gy')
- fine_mass: float32 [2048, 4096], P(('gx', 'gy'))
The draws below stay inside these ranges and needn't reach their ends.
Inputs may be any that keep to these rules, and one draw needn't show every extreme that they name: `halo_refined_cells`: each of the three coordinates (c // 256, c // 16 mod 16, c mod 16) is at most 14. `virt_cells`: the first coordinate is at most 14 and the second at most 30.
All inputs are finite; a program needn't handle non-finite values.
Results may differ from the reference program's by a relative error of at most 0.004.
Values may be sent and summed in bfloat16 or wider, within the bound.
No kernel may reach another device: no remote copies, remote signals or barrier semaphores. Data moves between devices by JAX's collectives and lax.ppermute only.
A program may use at most 128 MiB of HBM per device.

```python
import jax
import jax.numpy as jnp
from jax import lax

CX = 16
CY = 32
CZ = 128
PT = 128
FPD = 16
CAPP = 2048
VCAP = 512
RANKS = 128
NX = 128
NY = 512
NTX = 16
NTY = 64
NTZ = 16
FPATCH = 2048
N_GX = 8
N_GY = 16


def filled_counts(key, shape, most):
    first, second = jax.random.split(key)
    counts = jax.random.randint(first, shape, 0, most + 1)
    total = 1
    for extent in shape:
        total = total * extent
    chosen = jax.random.randint(second, (), 0, total)
    flat = jnp.arange(total, dtype=jnp.int32).reshape(shape)
    return jnp.where(flat == chosen, most, counts).astype(jnp.int32)


def draw_halo_refined_cells(key, part):
    key = jax.random.fold_in(key, 11)
    first, second, third = jax.random.split(key, 3)
    shape = (RANKS, 9, FPD, CAPP)
    along_x = jax.random.randint(first, shape, 0, 15)
    along_y = jax.random.randint(second, shape, 0, 15)
    depth_direction = jax.random.randint(third, shape, 0, 15)
    return (along_x * 256 + along_y * 16 + depth_direction).astype(jnp.int32)


def draw_virt_cells(key, part):
    key = jax.random.fold_in(key, 23)
    first, second, third = jax.random.split(key, 3)
    shape = (RANKS, 9, VCAP)
    along_x = jax.random.randint(first, shape, 0, CX - 1)
    along_y = jax.random.randint(second, shape, 0, CY - 1)
    depth_direction = jax.random.randint(third, shape, 0, CZ)
    return ((along_x * CY + along_y) * CZ + depth_direction).astype(jnp.int32)


def draw_ghost_counts(key, part):
    key = jax.random.fold_in(key, 37)
    return filled_counts(key, (RANKS, 9, FPD), CAPP)


def draw_phantom_slot_counts(key, part):
    key = jax.random.fold_in(key, 41)
    return filled_counts(key, (RANKS, 9), VCAP)


def set_ends(array, stream_key, least, high):
    longest = array.shape.index(max(array.shape))
    spots = []
    for shift in (0, 1):
        where = [jax.random.randint(jax.random.fold_in(stream_key, axis), (), 0, length) for axis, length in enumerate(array.shape)]
        where[longest] = (where[longest] + shift) % array.shape[longest]
        spots.append(tuple(where))
    return array.at[spots[0]].set(least).at[spots[1]].set(high)


def level_of(rng, dims, shards, least, top_value):
    factor_of, own = 1.0, jax.random.fold_in(rng, 6)
    for dim, shards_of in shards:
        steps = jnp.exp(jax.random.uniform(jax.random.fold_in(own, dim), (shards_of,), jnp.float32, least / len(shards), top_value / len(shards)))
        factor_of = factor_of * jnp.repeat(steps, dims[dim] // shards_of).reshape([-1 if axis == dim else 1 for axis in range(len(dims))])
    return factor_of


def setup_inputs(seed: int = 0) -> dict:
    arg_keys = jax.random.split(jax.random.key(seed), 10)
    return {
        "part_data": jnp.clip(1.0 * jax.random.uniform(arg_keys[0], (NTX, NTY, NTZ, 4, PT), jnp.float32) ** level_of(arg_keys[0], (NTX, NTY, NTZ, 4, PT), ((0, 8), (1, 16)), -0.2, 0.2), 0.0, 1.0).astype(jnp.bfloat16),
        "tile_cells": set_ends(jax.random.randint(arg_keys[1], (NTX, NTY, NTZ, PT), 0, 512), jax.random.fold_in(arg_keys[1], 1), 0, 511).astype(jnp.int32),
        "tile_counts": set_ends(jax.random.randint(arg_keys[2], (NTX, NTY, NTZ), PT // 4, PT + 1), jax.random.fold_in(arg_keys[2], 1), PT // 4, PT).astype(jnp.int32),
        "ghost_data": jnp.clip(1.0 * jax.random.uniform(arg_keys[3], (RANKS, 9, FPD, 4, CAPP), jnp.float32) ** level_of(arg_keys[3], (RANKS, 9, FPD, 4, CAPP), ((0, 128),), -0.2, 0.2), 0.0, 1.0).astype(jnp.bfloat16),
        "halo_refined_cells": draw_halo_refined_cells(jax.random.fold_in(arg_keys[9], 71), 0),
        "ghost_counts": draw_ghost_counts(jax.random.fold_in(arg_keys[9], 71), 0),
        "virt_data": jnp.clip(1.0 * jax.random.uniform(arg_keys[6], (RANKS, 9, 4, VCAP), jnp.float32) ** level_of(arg_keys[6], (RANKS, 9, 4, VCAP), ((0, 128),), -0.2, 0.2), 0.0, 1.0).astype(jnp.bfloat16),
        "virt_cells": draw_virt_cells(jax.random.fold_in(arg_keys[9], 71), 0),
        "phantom_slot_counts": draw_phantom_slot_counts(jax.random.fold_in(arg_keys[9], 71), 0),
    }


def corner_terms(fx, fy, fz, mass):
    fx32 = fx.astype(jnp.float32)
    fy32 = fy.astype(jnp.float32)
    fz32 = fz.astype(jnp.float32)
    low_x = lax.optimization_barrier((1.0 - fx32).astype(jnp.bfloat16)).astype(jnp.float32)
    low_y = lax.optimization_barrier((1.0 - fy32).astype(jnp.bfloat16)).astype(jnp.float32)
    along_x = jnp.stack([low_x, fx32], axis=-1)
    along_y = jnp.stack([low_y, fy32], axis=-1)
    depth_direction = jnp.stack([(1.0 - fz32) * mass, fz32 * mass], axis=-1)
    depth_direction = lax.optimization_barrier(depth_direction.astype(jnp.bfloat16)).astype(jnp.float32)
    sheet_layer = along_y[..., :, None] * depth_direction[..., None, :]
    sheet_layer = lax.optimization_barrier(sheet_layer.astype(jnp.bfloat16)).astype(jnp.float32)
    return along_x[..., :, None, None] * sheet_layer[..., None, :, :]


def reference(part_data, tile_cells, tile_counts, ghost_data, halo_refined_cells, ghost_counts, virt_data, virt_cells, phantom_slot_counts):
    offs_i = jnp.arange(2, dtype=jnp.int32).reshape(2, 1, 1)
    offs_j = jnp.arange(2, dtype=jnp.int32).reshape(1, 2, 1)
    offs_k = jnp.arange(2, dtype=jnp.int32).reshape(1, 1, 2)
    live = jnp.arange(PT, dtype=jnp.int32)[None, None, None, :] < tile_counts[..., None]
    mass = part_data[..., 0, :].astype(jnp.float32) * live.astype(jnp.float32)
    values = corner_terms(part_data[..., 1, :], part_data[..., 2, :], part_data[..., 3, :], mass)
    tile_x = jnp.arange(NTX, dtype=jnp.int32).reshape(NTX, 1, 1, 1)
    tile_y = jnp.arange(NTY, dtype=jnp.int32).reshape(1, NTY, 1, 1)
    tile_z = jnp.arange(NTZ, dtype=jnp.int32).reshape(1, 1, NTZ, 1)
    pos_x = (tile_x * 8 + tile_cells // 64)[..., None, None, None]
    pos_y = (tile_y * 8 + (tile_cells // 8) % 8)[..., None, None, None]
    pos_z = (tile_z * 8 + tile_cells % 8)[..., None, None, None]
    index = (((pos_x + offs_i) % NX) * NY + (pos_y + offs_j) % NY) * CZ + (pos_z + offs_k) % CZ
    base = jax.ops.segment_sum(values.reshape(-1), index.reshape(-1), num_segments=NX * NY * CZ)

    vlive = jnp.arange(VCAP, dtype=jnp.int32)[None, None, :] < phantom_slot_counts[..., None]
    vmass = virt_data[:, :, 0, :].astype(jnp.float32) * vlive.astype(jnp.float32)
    vvalues = corner_terms(virt_data[:, :, 1, :], virt_data[:, :, 2, :], virt_data[:, :, 3, :], vmass)
    source = jnp.arange(RANKS, dtype=jnp.int32).reshape(RANKS, 1, 1)
    offset = jnp.arange(9, dtype=jnp.int32).reshape(1, 9, 1)
    dest_x = (source // N_GY + offset // 3 - 1) % N_GX
    dest_y = (source % N_GY + offset % 3 - 1) % N_GY
    vx = (dest_x * CX + virt_cells // (CY * CZ))[..., None, None, None]
    vy = (dest_y * CY + (virt_cells // CZ) % CY)[..., None, None, None]
    vz = (virt_cells % CZ)[..., None, None, None]
    vindex = ((vx + offs_i) * NY + vy + offs_j) * CZ + (vz + offs_k) % CZ
    base = base + jax.ops.segment_sum(vvalues.reshape(-1), vindex.reshape(-1), num_segments=NX * NY * CZ)
    base_mass = base.reshape(NX, NY, CZ)

    def owner_patches(dest):
        own_x = dest // N_GY
        own_y = dest % N_GY
        offs = jnp.arange(9, dtype=jnp.int32)
        src_x = (own_x - (offs // 3 - 1)) % N_GX
        src_y = (own_y - (offs % 3 - 1)) % N_GY
        src = (src_x * N_GY + src_y).astype(jnp.int32)
        data = ghost_data[src, offs]
        cells = halo_refined_cells[src, offs]
        counts = ghost_counts[src, offs]
        glive = jnp.arange(CAPP, dtype=jnp.int32)[None, None, :] < counts[..., None]
        gmass = data[:, :, 0, :].astype(jnp.float32) * glive.astype(jnp.float32)
        gvalues = corner_terms(data[:, :, 1, :], data[:, :, 2, :], data[:, :, 3, :], gmass)
        patch = jnp.arange(FPD, dtype=jnp.int32).reshape(1, FPD, 1, 1, 1, 1)
        gx_pos = (cells // 256)[..., None, None, None]
        gy_pos = ((cells // 16) % 16)[..., None, None, None]
        gz_pos = (cells % 16)[..., None, None, None]
        gindex = patch * 4096 + (gx_pos + offs_i) * 256 + (gy_pos + offs_j) * 16 + gz_pos + offs_k
        summed = jax.ops.segment_sum(gvalues.reshape(-1), gindex.reshape(-1), num_segments=FPD * 4096)
        return summed.reshape(FPD, 4096)

    fine = lax.map(owner_patches, jnp.arange(RANKS, dtype=jnp.int32))
    fine_mass = fine.reshape(FPATCH, 4096)
    return base_mass, fine_mass
```

```python
import functools

import jax
import jax.numpy as jnp
from jax import lax
from jax.experimental import pallas as pl
from jax.experimental.pallas import tpu as pltpu
from jax.sharding import PartitionSpec as P

BF16 = jnp.bfloat16
F32 = jnp.float32
I32 = jnp.int32
NT = (((1,), (1,)), ((), ()))
LANES = 256
UNROLL = 16
PATCHES = 48
VMEM_LIMIT = 56 * 2**20


def shift(x, axis, by):
    devices = lax.axis_size(axis)
    return lax.ppermute(x, axis, [(i, (i + by) % devices) for i in range(devices)])


def sublane(rows, lanes):
    return lax.broadcasted_iota(I32, (rows, lanes), 0).astype(F32)


def dot_nt(a, b):
    return lax.dot_general(a, b, NT, preferred_element_type=F32)


def row8(ref, row):
    return ref[pl.ds(row, 8, stride=0), :]


def row16(ref, row):
    return jnp.concatenate([row8(ref, row)] * 2, 0).astype(BF16)


def fine_kernel(base_group, counts, data, cells, out, total, fields, partial):
    total[...] = jnp.zeros_like(total)
    partial[...] = jnp.zeros_like(partial)

    def chunks(group):
        return jnp.maximum((counts[base_group + group] + (LANES - 1)) >> 8, 1)

    work = lax.fori_loop(
        0, PATCHES, lambda group, t: t + chunks(group), jnp.int32(0), unroll=8
    )
    steps = lax.div(work + (UNROLL - 1), UNROLL)
    lane = lax.broadcasted_iota(I32, (1, LANES), 1)
    here = sublane(16, LANES).astype(BF16)
    before = (sublane(16, LANES) - 1.0).astype(BF16)
    rows = sublane(8, LANES)
    zero = jnp.zeros((16, LANES), BF16)

    def deposit(unit, group, chunk):
        patch = jnp.minimum(group, PATCHES - 1)
        live = jnp.where(group < PATCHES, counts[base_group + patch], 0)
        start = pl.multiple_of(chunk * LANES, LANES)
        high = data[patch, :, pl.ds(start, LANES)].astype(F32)
        cell = cells[pl.ds(patch, 1), pl.ds(start, LANES)]
        low = 1.0 - high
        mass = jnp.where(lane < live - start, high[0:1], 0.0)
        f = fields.at[unit]
        f[0:4, :] = high
        f[4:8, :] = low
        f[8:9, :] = high[3:4] * mass
        f[9:10, :] = low[3:4] * mass
        f[10:11, :] = (cell >> 8).astype(F32)
        f[11:12, :] = (cell & 15).astype(F32)
        f[12:13, :] = ((cell >> 4) & 3).astype(F32)
        f[13:14, :] = ((cell >> 6) & 3).astype(F32)
        inner = row8(f, 12)
        f[16:24, :] = jnp.where(
            rows == inner, row8(f, 6), jnp.where(rows - 1.0 == inner, row8(f, 2), 0.0)
        )
        x, outer, z = row16(f, 10), row16(f, 13), row16(f, 11)
        along_x = jnp.where(here == x, row16(f, 5), jnp.where(before == x, row16(f, 1), zero))
        along_z = jnp.where(here == z, row16(f, 9), jnp.where(before == z, row16(f, 8), zero))
        left = jnp.concatenate(
            [jnp.where(outer == BF16(k), along_x, zero) for k in range(4)], 0
        )
        right = jnp.concatenate([row16(f, 16 + k) * along_z for k in range(5)], 0)
        partial[unit, :, 0:80] = dot_nt(left, right)
        last = chunk + 1 >= chunks(patch)
        return patch, jnp.where(last, group + 1, group), jnp.where(last, 0, chunk + 1)

    def body(_, carry):
        group, chunk, *old = carry
        new = []
        for unit in range(UNROLL):
            total[old[unit]] += partial[unit]
            patch, group, chunk = deposit(unit, group, chunk)
            new.append(patch)
        return (group, chunk, *new)

    carry = lax.fori_loop(0, steps, body, (jnp.int32(0),) * (UNROLL + 2))
    for unit in range(UNROLL):
        total[carry[2 + unit]] += partial[unit]
    lane = lax.broadcasted_iota(I32, (16, 128), 1)

    def fold(group, _):
        for half in range(2):
            at = 32 * half
            even = total[group, at : at + 16]
            odd = total[group, at + 16 : at + 32]
            prior = total[group, at - 16 : at] if half else jnp.zeros((16, 128), F32)
            swapped = pltpu.roll(jnp.where(lane < 64, odd, prior), 64, 1)
            out[group, 16 * half : 16 * half + 16] = (even + swapped).astype(BF16)
        return 0

    lax.fori_loop(0, PATCHES, fold, 0, unroll=8)


def fine_part(part, counts, data, cells):
    slots = data.shape[2]
    return pl.pallas_call(
        functools.partial(fine_kernel, PATCHES * part),
        grid_spec=pltpu.PrefetchScalarGridSpec(
            num_scalar_prefetch=1,
            grid=(1,),
            in_specs=[
                pl.BlockSpec((PATCHES, 4, slots), lambda i, c: (part, 0, 0)),
                pl.BlockSpec((PATCHES, slots), lambda i, c: (part, 0)),
            ],
            out_specs=pl.BlockSpec((PATCHES, 32, 128), lambda i, c: (0, 0, 0)),
            scratch_shapes=[
                pltpu.VMEM((PATCHES, 64, 128), F32),
                pltpu.VMEM((UNROLL, 24, LANES), F32),
                pltpu.VMEM((UNROLL, 64, 128), F32),
            ],
        ),
        out_shape=jax.ShapeDtypeStruct((PATCHES, 32, 128), BF16),
        compiler_params=pltpu.CompilerParams(vmem_limit_bytes=VMEM_LIMIT),
        cost_estimate=pl.CostEstimate(
            flops=2 * PATCHES * slots * 64 * 128, bytes_accessed=1600000, transcendentals=0
        ),
        name="fine",
    )(counts, data, cells)


def tile_kernel(
    counts, vcounts, data, cells, vdata, vcells, core, face_x, face_y, *rest
):
    packs, (grid, fields) = rest[:3], rest[3:]
    grid[...] = jnp.zeros_like(grid)
    lane = lax.broadcasted_iota(I32, (1, 512), 1)
    for offset in range(9):
        high = vdata[offset].astype(F32)
        pack = packs[offset // 3].at[offset % 3]
        pack[0:1, :] = jnp.where(lane < vcounts[offset], high[0:1], 0.0)
        pack[1:4, :] = high[1:4]
        pack[4:5, :] = vcells[offset : offset + 1, :].astype(F32)
        pack[5:8, :] = jnp.zeros((3, 512), F32)
    lane = lax.broadcasted_iota(I32, (1, 128), 1)
    here = sublane(16, LANES).astype(BF16)
    before = (sublane(16, LANES) - 1.0).astype(BF16)
    fifteen = (sublane(16, LANES) + 15.0).astype(BF16)
    rows = sublane(16, LANES)
    zero = jnp.zeros((16, LANES), BF16)

    def column(col, _):
        acc = jnp.zeros((144, 128), F32)
        for pair in range(8):
            tile = col * 16 + 2 * pair
            f = fields.at[pair]
            high = jnp.concatenate(
                [data[tile].astype(F32), data[tile + 1].astype(F32)], 1
            )
            low = 1.0 - high
            live = jnp.concatenate(
                [jnp.where(lane < counts[tile], 1.0, 0.0),
                 jnp.where(lane < counts[tile + 1], 1.0, 0.0)], 1
            )
            cell = jnp.concatenate(
                [cells[pl.ds(tile, 1), :], cells[pl.ds(tile + 1, 1), :] + 1024], 1
            )
            mass = high[0:1] * live
            f[0:4, :] = high
            f[4:8, :] = low
            f[8:9, :] = high[3:4] * mass
            f[9:10, :] = low[3:4] * mass
            f[10:11, :] = ((cell >> 6) & 7).astype(F32)
            f[11:12, :] = ((cell >> 3) & 7).astype(F32)
            f[12:13, :] = ((cell & 7) + ((cell >> 10) << 3)).astype(F32)
            x = jnp.concatenate([row8(f, 10)] * 2, 0)
            low_x = jnp.concatenate([row8(f, 5)] * 2, 0)
            high_x = jnp.concatenate([row8(f, 1)] * 2, 0)
            f[16:32, :] = jnp.where(
                rows == x, low_x, jnp.where(rows - 1.0 == x, high_x, 0.0)
            )
            y, z = row16(f, 11), row16(f, 12)
            c0, c1 = row16(f, 9), row16(f, 8)
            along_y = jnp.where(
                here == y, row16(f, 6), jnp.where(before == y, row16(f, 2), zero)
            )
            along_z = jnp.concatenate(
                [jnp.where(here == z, c0, jnp.where(before == z, c1, zero)),
                 jnp.where(fifteen == z, c1, zero)], 0
            )
            left = jnp.concatenate([row16(f, 16 + k) * along_y for k in range(9)], 0)
            part = jnp.concatenate(
                [dot_nt(left, along_z), jnp.zeros((144, 96), F32)], 1
            )
            acc = acc + (pltpu.roll(part, 16 * pair, 1) if pair else part)
        tx = col >> 2
        ty = col & 3
        for k in range(9):
            grid[8 * tx + k, pl.ds(pl.multiple_of(8 * ty, 8), 16), :] += acc[
                16 * k : 16 * k + 16
            ]
        return 0

    lax.fori_loop(0, 8, column, 0)
    core[...] = grid[0:16, 0:32, :]
    face_x[...] = grid[16]
    face_y[...] = grid[0:16, 32, :]


def tile_part(counts, vcounts, data, cells, vdata, vcells):
    full = pl.BlockSpec(memory_space=pltpu.VMEM)
    smem = pl.BlockSpec(memory_space=pltpu.SMEM)
    return pl.pallas_call(
        tile_kernel,
        in_specs=[smem, smem, full, full, full, full],
        out_specs=[full] * 6,
        out_shape=[
            jax.ShapeDtypeStruct((16, 32, 128), F32),
            jax.ShapeDtypeStruct((40, 128), F32),
            jax.ShapeDtypeStruct((16, 128), F32),
        ]
        + [jax.ShapeDtypeStruct((3, 8, 512), F32)] * 3,
        scratch_shapes=[
            pltpu.VMEM((17, 40, 128), F32),
            pltpu.VMEM((8, 32, LANES), F32),
        ],
        compiler_params=pltpu.CompilerParams(vmem_limit_bytes=VMEM_LIMIT),
        name="tiles",
    )(counts, vcounts, data, cells, vdata, vcells)


def base_kernel(pack_own, pack_up, pack_down, core, from_x, from_y, out, fields):
    out[...] = core[...].reshape(512, 128)
    out[0:32, :] += from_x[0:32, :]
    for x in range(16):
        out[32 * x : 32 * x + 1, :] += from_y[x : x + 1, :]
    lanes = 512
    rows = sublane(16, lanes)
    zero = jnp.zeros((16, lanes), BF16)

    def place(at):
        return (rows + float(at)).astype(BF16)

    def one(source, index):
        f = fields
        high = source[index, 0:4, :]
        low = 1.0 - high
        cell = source[index, 4:5, :].astype(I32)
        mass = high[0:1]
        f[0:4, :] = high
        f[4:8, :] = low
        f[8:9, :] = high[3:4] * mass
        f[9:10, :] = low[3:4] * mass
        f[10:11, :] = (cell >> 12).astype(F32)
        f[11:12, :] = ((cell >> 7) & 31).astype(F32)
        f[12:13, :] = (cell & 127).astype(F32)
        f[13:14, :] = ((cell + 1) & 127).astype(F32)
        x = jnp.concatenate([row8(f, 10)] * 2, 0)
        low_x = jnp.concatenate([row8(f, 5)] * 2, 0)
        high_x = jnp.concatenate([row8(f, 1)] * 2, 0)
        f[16:32, :] = jnp.where(
            rows == x, low_x, jnp.where(rows - 1.0 == x, high_x, 0.0)
        )
        y, z, z_next = row16(f, 11), row16(f, 12), row16(f, 13)
        c0, c1 = row16(f, 9), row16(f, 8)
        y0, y1 = row16(f, 6), row16(f, 2)
        along_y = [
            jnp.where(place(16 * h) == y, y0, jnp.where(place(16 * h - 1) == y, y1, zero))
            for h in range(2)
        ]
        along_z = jnp.concatenate(
            [
                jnp.where(
                    place(16 * k) == z, c0, jnp.where(place(16 * k) == z_next, c1, zero)
                )
                for k in range(8)
            ],
            0,
        )
        left = []
        for k in range(16):
            w = row16(f, 16 + k)
            left += [w * along_y[0], w * along_y[1]]
        out[...] += dot_nt(jnp.concatenate(left, 0), along_z)

    for source in (pack_own, pack_up, pack_down):
        def body(index, _, source=source):
            one(source, index)
            return 0
        lax.fori_loop(0, 3, body, 0)


def base_part(*args):
    full = pl.BlockSpec(memory_space=pltpu.VMEM)
    return pl.pallas_call(
        base_kernel,
        in_specs=[full] * 6,
        out_specs=full,
        out_shape=jax.ShapeDtypeStruct((512, 128), F32),
        scratch_shapes=[pltpu.VMEM((32, 512), F32)],
        compiler_params=pltpu.CompilerParams(vmem_limit_bytes=VMEM_LIMIT),
        cost_estimate=pl.CostEstimate(
            flops=2 * 9 * 512 * 512 * 128, bytes_accessed=1000000, transcendentals=0
        ),
        name="base",
    )(*args)


def sum_kernel(own, left, right, up, down, out, lines):
    for patch in range(16):
        mass = (
            (own[patch].astype(F32) + left[patch].astype(F32))
            + (right[patch].astype(F32) + up[patch].astype(F32))
        ) + down[patch].astype(F32)
        lines[32 * patch : 32 * patch + 32, :] = mass
    for group in range(2):
        for half in range(2):
            for x in range(16):
                block = lines[pl.ds(256 * group + 16 * half + x, 8, stride=32), :]
                at = 128 * (2 * x + half)
                out[8 * group : 8 * group + 8, at : at + 128] = block


def sum_part(own, left, right, up, down):
    part = pl.BlockSpec((16, 32, 128), lambda i: (1, 0, 0))
    full = pl.BlockSpec((16, 32, 128), lambda i: (0, 0, 0))
    return pl.pallas_call(
        sum_kernel,
        grid=(1,),
        in_specs=[part, part, part, full, full],
        out_specs=pl.BlockSpec((16, 4096), lambda i: (0, 0)),
        out_shape=jax.ShapeDtypeStruct((16, 4096), F32),
        scratch_shapes=[pltpu.VMEM((512, 128), F32)],
        compiler_params=pltpu.CompilerParams(vmem_limit_bytes=VMEM_LIMIT),
        name="patches",
    )(own, left, right, up, down)


def on_device(
    part_data,
    tile_cells,
    tile_counts,
    ghost_data,
    halo_refined_cells,
    ghost_counts,
    virt_data,
    virt_cells,
    phantom_slot_counts,
):
    core, face_x, face_y, pack_m, pack_0, pack_p = tile_part(
        tile_counts.reshape(128),
        phantom_slot_counts.reshape(9),
        part_data.reshape(128, 4, 128),
        tile_cells.reshape(128, 128),
        virt_data.reshape(9, 4, 512),
        virt_cells.reshape(9, 512),
    )
    counts = ghost_counts.reshape(144)
    data = ghost_data.reshape(144, 4, 2048)
    cells = halo_refined_cells.reshape(144, 2048)

    pack_r = shift(pack_m, "gx", -1)
    pack_l = shift(pack_p, "gx", 1)
    from_x = shift(face_x, "gx", 1)
    fine_m = fine_part(0, counts, data, cells)
    fine_r = shift(fine_m, "gx", -1)

    pack_all = jnp.stack([pack_0, pack_r, pack_l])
    pack_up = shift(pack_all[:, 0], "gy", -1)
    pack_down = shift(pack_all[:, 2], "gy", 1)
    from_y = shift(face_y.at[0].add(from_x[32]), "gy", 1)
    fine_p = fine_part(2, counts, data, cells)
    fine_l = shift(fine_p, "gx", 1)
    fine_0 = fine_part(1, counts, data, cells)

    def joint(at):
        part = slice(16 * at, 16 * at + 16)
        return (
            fine_0[part].astype(F32) + fine_r[part].astype(F32) + fine_l[part].astype(F32)
        ).astype(BF16)

    up = shift(joint(0), "gy", -1)
    down = shift(joint(2), "gy", 1)
    base = base_part(pack_all[:, 1], pack_up, pack_down, core, from_x, from_y)
    fine_mass = sum_part(fine_0, fine_r, fine_l, up, down)
    return base.reshape(16, 32, 128), fine_mass


def solution(mesh):
    return jax.shard_map(
        on_device,
        mesh=mesh,
        in_specs=(
            P("gx", "gy", None, None, None),
            P("gx", "gy", None, None),
            P("gx", "gy", None),
            P(("gx", "gy"), None, None, None, None),
            P(("gx", "gy"), None, None, None),
            P(("gx", "gy"), None, None),
            P(("gx", "gy"), None, None, None),
            P(("gx", "gy"), None, None),
            P(("gx", "gy"), None),
        ),
        out_specs=(P("gx", "gy", None), P(("gx", "gy"), None)),
        check_vma=False,
    )
```

```python
import functools

import jax
import jax.numpy as jnp
from jax import lax
from jax.experimental import pallas as pl
from jax.experimental.pallas import tpu as pltpu
from jax.sharding import PartitionSpec as P

BF16 = jnp.bfloat16
F32 = jnp.float32
I32 = jnp.int32
NT = (((1,), (1,)), ((), ()))
LANES = 256
UNROLL = 16
PATCHES = 48
VMEM_LIMIT = 56 * 2**20


def shift(x, axis, by):
    devices = lax.axis_size(axis)
    return lax.ppermute(x, axis, [(i, (i + by) % devices) for i in range(devices)])


def sublane(rows, lanes):
    return lax.broadcasted_iota(I32, (rows, lanes), 0).astype(F32)


def dot_nt(a, b):
    return lax.dot_general(a, b, NT, preferred_element_type=F32)


def row8(ref, row):
    return ref[pl.ds(row, 8, stride=0), :]


def row16(ref, row):
    return jnp.concatenate([row8(ref, row)] * 2, 0).astype(BF16)


def high_low(x):
    high = x.astype(BF16)
    return high, (x - high.astype(F32)).astype(BF16)


def pack_virtual(offset, counts, data, cells, lines):
    lane = lax.broadcasted_iota(I32, (1, 512), 1)
    high = data[0, offset].astype(F32)
    cell = cells[0, offset : offset + 1, :]
    values = [
        jnp.where(lane < counts[0, offset], high[0:1], 0.0),
        high[1:2],
        high[2:3],
        high[3:4],
        (cell >> 8).astype(F32),
        (cell & 255).astype(F32),
    ]
    for field, value in enumerate(values):
        for quarter in range(4):
            at = 4 * field + quarter
            lines[at : at + 1, :] = value[:, 128 * quarter : 128 * quarter + 128]
    lines[24:32, :] = jnp.zeros((8, 128), F32)
    return lines[...].astype(BF16)


def fine_kernel(offsets, split, counts, vcounts, data_hbm, cells_hbm, vdata, vcells, face, wait, *rest):
    outs, rest = rest[:split], rest[split:]
    data, cells, total, fields, partial, lines, number, sems = rest
    patches = 16 * len(offsets)
    copies = []
    for at, offset in enumerate(offsets):
        copies.append(
            pltpu.make_async_copy(
                data_hbm.at[0, offset], data.at[pl.ds(16 * at, 16)], sems.at[2 * at]
            )
        )
        copies.append(
            pltpu.make_async_copy(
                cells_hbm.at[0, offset], cells.at[pl.ds(16 * at, 16)], sems.at[2 * at + 1]
            )
        )
    for copy in copies:
        copy.start()
    total[...] = jnp.zeros_like(total)
    partial[...] = jnp.zeros_like(partial)
    work = jnp.int32(0)
    for at, offset in enumerate(offsets):
        for patch in range(16):
            live = counts[0, offset, patch]
            number[16 * at + patch] = live
            work = work + jnp.maximum((live + (LANES - 1)) >> 8, 1)
    for extra in range(UNROLL + 4):
        number[patches + extra] = 0
    steps = lax.div(work + (UNROLL - 1), UNROLL)
    each = len(offsets) // split
    for index, offset in enumerate(offsets):
        slot = 17 * (index % each) + 16
        outs[index // each][slot] = pack_virtual(offset, vcounts, vdata, vcells, lines)
    if len(offsets) == 6:
        high, low = high_low(face[...])
        outs[1][51] = high[0:32]
        outs[1][52] = low[0:32]
        high, low = high_low(jnp.concatenate([face[32:40, :], jnp.zeros((8, 128), F32)], 0))
        outs[1][53] = jnp.concatenate([high, low], 0)
    lane = lax.broadcasted_iota(I32, (1, LANES), 1)
    here = sublane(16, LANES).astype(BF16)
    before = (sublane(16, LANES) - 1.0).astype(BF16)
    rows = sublane(8, LANES)
    zero = jnp.zeros((16, LANES), BF16)
    for copy in copies:
        copy.wait()

    def deposit(unit, group, start, live, next_one, next_two):
        patch = jnp.minimum(group, patches - 1)
        at = pl.multiple_of(start, LANES)
        high = data[patch, :, pl.ds(at, LANES)].astype(F32)
        cell = cells[pl.ds(patch, 1), pl.ds(at, LANES)]
        low = 1.0 - high
        mass = jnp.where(lane < live, high[0:1], 0.0)
        f = fields.at[unit]
        f[0:4, :] = high
        f[4:8, :] = low
        f[8:9, :] = high[3:4] * mass
        f[9:10, :] = low[3:4] * mass
        f[10:11, :] = (cell >> 8).astype(F32)
        f[11:12, :] = (cell & 15).astype(F32)
        f[12:13, :] = ((cell >> 4) & 3).astype(F32)
        f[13:14, :] = ((cell >> 6) & 3).astype(F32)
        inner = row8(f, 12)
        f[16:24, :] = jnp.where(
            rows == inner, row8(f, 6), jnp.where(rows - 1.0 == inner, row8(f, 2), 0.0)
        )
        x, outer, z = row16(f, 10), row16(f, 13), row16(f, 11)
        along_x = jnp.where(here == x, row16(f, 5), jnp.where(before == x, row16(f, 1), zero))
        along_z = jnp.where(here == z, row16(f, 9), jnp.where(before == z, row16(f, 8), zero))
        left = jnp.concatenate(
            [jnp.where(outer == BF16(k), along_x, zero) for k in range(4)], 0
        )
        right = jnp.concatenate([row16(f, 16 + k) * along_z for k in range(5)], 0)
        partial[unit, :, 0:80] = dot_nt(left, right)
        last = live <= LANES
        group = jnp.where(last, group + 1, group)
        return patch, (
            group,
            jnp.where(last, 0, start + LANES),
            jnp.where(last, next_one, live - LANES),
            jnp.where(last, next_two, next_one),
            number[group + 2],
        )

    def body(_, carry):
        state, old = carry[:5], carry[5:]
        new = []
        for unit in range(UNROLL):
            total[old[unit]] += partial[unit]
            patch, state = deposit(unit, *state)
            new.append(patch)
        return (*state, *new)

    none = jnp.int32(0)
    carry = lax.fori_loop(
        0, steps, body, (none, none, number[0], number[1], number[2]) + (none,) * UNROLL
    )
    for unit in range(UNROLL):
        total[carry[5 + unit]] += partial[unit]
    lane = lax.broadcasted_iota(I32, (16, 128), 1)

    for index in range(split):
        out = outs[index]

        def fold(k, _, index=index, out=out):
            group = 16 * each * index + k
            for half in range(2):
                at = 32 * half
                even = total[group, at : at + 16]
                odd = total[group, at + 16 : at + 32]
                prior = total[group, at - 16 : at] if half else jnp.zeros((16, 128), F32)
                swapped = pltpu.roll(jnp.where(lane < 64, odd, prior), 64, 1)
                out[k + (k >> 4), 16 * half : 16 * half + 16] = (even + swapped).astype(BF16)
            return 0

        lax.fori_loop(0, 16 * each, fold, 0, unroll=8)


def fine_part(offsets, sizes, counts, vcounts, data, cells, vdata, vcells, face, wait):
    slots = data.shape[4]
    patches = 16 * len(offsets)
    full = pl.BlockSpec(memory_space=pltpu.VMEM)
    smem = pl.BlockSpec(memory_space=pltpu.SMEM)
    anywhere = pl.BlockSpec(memory_space=pl.ANY)
    return pl.pallas_call(
        functools.partial(fine_kernel, offsets, len(sizes)),
        in_specs=[smem, smem, anywhere, anywhere, full, full, full, anywhere],
        out_specs=[full] * len(sizes),
        scratch_shapes=[
            pltpu.VMEM((patches, 4, slots), BF16),
            pltpu.VMEM((patches, slots), I32),
            pltpu.VMEM((patches, 64, 128), F32),
            pltpu.VMEM((UNROLL, 24, LANES), F32),
            pltpu.VMEM((UNROLL, 64, 128), F32),
            pltpu.VMEM((32, 128), F32),
            pltpu.SMEM((patches + UNROLL + 4,), I32),
            pltpu.SemaphoreType.DMA((2 * len(offsets),)),
        ],
        out_shape=[jax.ShapeDtypeStruct((size, 32, 128), BF16) for size in sizes],
        compiler_params=pltpu.CompilerParams(vmem_limit_bytes=VMEM_LIMIT),
        cost_estimate=pl.CostEstimate(
            flops=4 * patches * slots * 64 * 128, bytes_accessed=40000 * patches, transcendentals=0
        ),
        name="fine",
    )(counts, vcounts, data, cells, vdata, vcells, face, wait)


def tile_kernel(counts, data, cells, core, face_x, face_y, grid, fields):
    grid[...] = jnp.zeros_like(grid)
    lane = lax.broadcasted_iota(I32, (1, 128), 1)
    here = sublane(16, LANES).astype(BF16)
    before = (sublane(16, LANES) - 1.0).astype(BF16)
    fifteen = (sublane(16, LANES) + 15.0).astype(BF16)
    rows = sublane(16, LANES)
    zero = jnp.zeros((16, LANES), BF16)

    def column(col, _):
        tx = col >> 2
        ty = col & 3
        acc = jnp.zeros((144, 128), F32)
        for pair in range(8):
            tz = 2 * pair
            f = fields.at[pair]
            high = jnp.concatenate(
                [data[tx, ty, tz].astype(F32), data[tx, ty, tz + 1].astype(F32)], 1
            )
            low = 1.0 - high
            live = jnp.concatenate(
                [jnp.where(lane < counts[tx, ty, tz], 1.0, 0.0),
                 jnp.where(lane < counts[tx, ty, tz + 1], 1.0, 0.0)], 1
            )
            cell = jnp.concatenate(
                [cells[tx, ty, tz : tz + 1, :], cells[tx, ty, tz + 1 : tz + 2, :] + 1024], 1
            )
            mass = high[0:1] * live
            f[0:4, :] = high
            f[4:8, :] = low
            f[8:9, :] = high[3:4] * mass
            f[9:10, :] = low[3:4] * mass
            f[10:11, :] = ((cell >> 6) & 7).astype(F32)
            f[11:12, :] = ((cell >> 3) & 7).astype(F32)
            f[12:13, :] = ((cell & 7) + ((cell >> 10) << 3)).astype(F32)
            x = jnp.concatenate([row8(f, 10)] * 2, 0)
            low_x = jnp.concatenate([row8(f, 5)] * 2, 0)
            high_x = jnp.concatenate([row8(f, 1)] * 2, 0)
            f[16:32, :] = jnp.where(
                rows == x, low_x, jnp.where(rows - 1.0 == x, high_x, 0.0)
            )
            y, z = row16(f, 11), row16(f, 12)
            c0, c1 = row16(f, 9), row16(f, 8)
            along_y = jnp.where(
                here == y, row16(f, 6), jnp.where(before == y, row16(f, 2), zero)
            )
            along_z = jnp.concatenate(
                [jnp.where(here == z, c0, jnp.where(before == z, c1, zero)),
                 jnp.where(fifteen == z, c1, zero)], 0
            )
            left = jnp.concatenate([row16(f, 16 + k) * along_y for k in range(9)], 0)
            part = jnp.concatenate(
                [dot_nt(left, along_z), jnp.zeros((144, 96), F32)], 1
            )
            acc = acc + (pltpu.roll(part, 16 * pair, 1) if pair else part)
        for k in range(9):
            grid[8 * tx + k, pl.ds(pl.multiple_of(8 * ty, 8), 16), :] += acc[
                16 * k : 16 * k + 16
            ]
        return 0

    lax.fori_loop(0, 8, column, 0)
    core[...] = grid[0:16, 0:32, :]
    face_x[...] = grid[16]
    face_y[...] = grid[0:16, 32, :]


def tile_part(counts, data, cells):
    full = pl.BlockSpec(memory_space=pltpu.VMEM)
    smem = pl.BlockSpec(memory_space=pltpu.SMEM)
    return pl.pallas_call(
        tile_kernel,
        in_specs=[smem, full, full],
        out_specs=[full] * 3,
        out_shape=[
            jax.ShapeDtypeStruct((16, 32, 128), F32),
            jax.ShapeDtypeStruct((40, 128), F32),
            jax.ShapeDtypeStruct((16, 128), F32),
        ],
        scratch_shapes=[
            pltpu.VMEM((17, 40, 128), F32),
            pltpu.VMEM((8, 32, LANES), F32),
        ],
        compiler_params=pltpu.CompilerParams(vmem_limit_bytes=VMEM_LIMIT),
        name="tiles",
    )(counts, data, cells)


def virtual_deposit(packs, out, lines, fields):
    lanes = 512
    rows = sublane(16, lanes)
    zero = jnp.zeros((16, lanes), BF16)

    def place(at):
        return (rows + float(at)).astype(BF16)

    for which, (source, slot) in enumerate(packs):
        f = fields.at[which & 1]
        g = lines.at[which & 1]
        g[...] = source[slot].astype(F32)

        def value(field):
            return jnp.concatenate(
                [g[4 * field + quarter : 4 * field + quarter + 1, :] for quarter in range(4)], 1
            )

        cell = (value(4) * 256.0 + value(5)).astype(I32)
        mass, fx, fy, fz = value(0), value(1), value(2), value(3)
        f[0:1, :] = fx
        f[1:2, :] = 1.0 - fx
        f[2:3, :] = fy
        f[3:4, :] = 1.0 - fy
        f[4:5, :] = fz * mass
        f[5:6, :] = (1.0 - fz) * mass
        f[10:11, :] = (cell >> 12).astype(F32)
        f[11:12, :] = ((cell >> 7) & 31).astype(F32)
        f[12:13, :] = (cell & 127).astype(F32)
        f[13:14, :] = ((cell + 1) & 127).astype(F32)
        x = jnp.concatenate([row8(f, 10)] * 2, 0)
        low_x = jnp.concatenate([row8(f, 1)] * 2, 0)
        high_x = jnp.concatenate([row8(f, 0)] * 2, 0)
        f[16:32, :] = jnp.where(
            rows == x, low_x, jnp.where(rows - 1.0 == x, high_x, 0.0)
        )
        y, z, z_next = row16(f, 11), row16(f, 12), row16(f, 13)
        c0, c1 = row16(f, 5), row16(f, 4)
        y0, y1 = row16(f, 3), row16(f, 2)
        along_y = [
            jnp.where(place(16 * h) == y, y0, jnp.where(place(16 * h - 1) == y, y1, zero))
            for h in range(2)
        ]
        along_z = jnp.concatenate(
            [
                jnp.where(
                    place(16 * k) == z, c0, jnp.where(place(16 * k) == z_next, c1, zero)
                )
                for k in range(8)
            ],
            0,
        )
        left = []
        for k in range(16):
            w = row16(f, 16 + k)
            left += [w * along_y[0], w * along_y[1]]
        out[...] += dot_nt(jnp.concatenate(left, 0), along_z)


def base_kernel(own, right, left, core, out, lines, fields):
    out[...] = core[...].reshape(512, 128)
    out[0:32, :] += left[51].astype(F32) + left[52].astype(F32)
    virtual_deposit([(own, 16), (right, 33), (left, 33)], out, lines, fields)


def base_part(*args):
    full = pl.BlockSpec(memory_space=pltpu.VMEM)
    return pl.pallas_call(
        base_kernel,
        in_specs=[full] * 4,
        out_specs=full,
        out_shape=jax.ShapeDtypeStruct((512, 128), F32),
        scratch_shapes=[pltpu.VMEM((2, 32, 128), F32), pltpu.VMEM((2, 32, 512), F32)],
        compiler_params=pltpu.CompilerParams(vmem_limit_bytes=VMEM_LIMIT),
        cost_estimate=pl.CostEstimate(
            flops=6 * 3 * 512 * 512 * 128, bytes_accessed=1000000, transcendentals=0
        ),
        name="base",
    )(*args)


def join_kernel(own, right, left, face_y, up, down):
    for at, (out, slot) in enumerate(((up, 0), (down, 34))):
        for patch in range(16):
            out[patch] = (
                own[17 * at + patch].astype(F32)
                + right[slot + patch].astype(F32)
                + left[slot + patch].astype(F32)
            ).astype(BF16)
        out[16] = own[17 * at + 16]
        out[17] = right[slot + 16]
        out[18] = left[slot + 16]
    corner = left[53].astype(F32)
    row = lax.broadcasted_iota(I32, (16, 128), 0)
    face = face_y[...] + jnp.where(row == 0, corner[0:16] + corner[16:32], 0.0)
    high, low = high_low(face)
    down[19] = jnp.concatenate([high, low], 0)


def join_part(*args):
    full = pl.BlockSpec(memory_space=pltpu.VMEM)
    return pl.pallas_call(
        join_kernel,
        in_specs=[full] * 4,
        out_specs=[full] * 2,
        out_shape=[jax.ShapeDtypeStruct((size, 32, 128), BF16) for size in (19, 20)],
        compiler_params=pltpu.CompilerParams(vmem_limit_bytes=VMEM_LIMIT),
        name="join",
    )(*args)


def last_kernel(part, own, right, left, up, down, base, out, patches, fields, lines):
    for patch in range(16):
        mass = (
            (own[patch].astype(F32) + left[17 + patch].astype(F32))
            + (right[17 + patch].astype(F32) + up[patch].astype(F32))
        ) + down[patch].astype(F32)
        patches[32 * patch : 32 * patch + 32, :] = mass
    for group in range(2):
        for half in range(2):
            for x in range(16):
                block = patches[pl.ds(256 * group + 16 * half + x, 8, stride=32), :]
                at = 128 * (2 * x + half)
                out[8 * group : 8 * group + 8, at : at + 128] = block
    base[...] = part[...]
    both = down[19].astype(F32)
    face = both[0:16] + both[16:32]
    for x in range(16):
        base[32 * x : 32 * x + 1, :] += face[x : x + 1, :]
    virtual_deposit(
        [(source, slot) for source in (up, down) for slot in (16, 17, 18)], base, lines, fields
    )


def last_part(*args):
    full = pl.BlockSpec(memory_space=pltpu.VMEM)
    return pl.pallas_call(
        last_kernel,
        in_specs=[full] * 6,
        out_specs=[full] * 2,
        out_shape=[
            jax.ShapeDtypeStruct((512, 128), F32),
            jax.ShapeDtypeStruct((16, 4096), F32),
        ],
        scratch_shapes=[
            pltpu.VMEM((512, 128), F32),
            pltpu.VMEM((2, 32, 512), F32),
            pltpu.VMEM((2, 32, 128), F32),
        ],
        compiler_params=pltpu.CompilerParams(vmem_limit_bytes=VMEM_LIMIT),
        name="last",
    )(*args)


def on_device(
    part_data,
    tile_cells,
    tile_counts,
    ghost_data,
    halo_refined_cells,
    ghost_counts,
    virt_data,
    virt_cells,
    phantom_slot_counts,
):
    core, face_x, face_y = tile_part(tile_counts, part_data, tile_cells)
    ghosts = (ghost_counts, phantom_slot_counts, ghost_data, halo_refined_cells)
    ghosts += (virt_data, virt_cells, face_x)
    toward, away = fine_part((0, 1, 2, 6, 7, 8), (51, 54), *ghosts, core)
    right = shift(toward, "gx", -1)
    left = shift(away, "gx", 1)
    (sides,) = fine_part((3, 5), (34,), *ghosts, away)
    up, down = join_part(sides, right, left, face_y)
    from_up = shift(up, "gy", -1)
    from_down = shift(down, "gy", 1)
    (own,) = fine_part((4,), (17,), *ghosts, down)
    part = base_part(own, right, left, core)
    base, fine_mass = last_part(part, own, right, left, from_up, from_down)
    return base.reshape(16, 32, 128), fine_mass


def solution(mesh):
    return jax.shard_map(
        on_device,
        mesh=mesh,
        in_specs=(
            P("gx", "gy", None, None, None),
            P("gx", "gy", None, None),
            P("gx", "gy", None),
            P(("gx", "gy"), None, None, None, None),
            P(("gx", "gy"), None, None, None),
            P(("gx", "gy"), None, None),
            P(("gx", "gy"), None, None, None),
            P(("gx", "gy"), None, None),
            P(("gx", "gy"), None),
        ),
        out_specs=(P("gx", "gy", None), P(("gx", "gy"), None)),
        check_vma=False,
    )
```

```python
import functools

import jax
import jax.numpy as jnp
from jax import lax
from jax.experimental import pallas as pl
from jax.experimental.pallas import tpu as pltpu
from jax.sharding import PartitionSpec as P

BF16 = jnp.bfloat16
F32 = jnp.float32
I32 = jnp.int32
NT = (((1,), (1,)), ((), ()))
LANES = 256
UNROLL = 32
PATCHES = 48
VMEM_LIMIT = 56 * 2**20
SMALL_LIMIT = 16 * 2**20


def shift(x, axis, by):
    devices = lax.axis_size(axis)
    return lax.ppermute(x, axis, [(i, (i + by) % devices) for i in range(devices)])


def sublane(rows, lanes):
    return lax.broadcasted_iota(I32, (rows, lanes), 0).astype(F32)


def dot_nt(a, b):
    return lax.dot_general(a, b, NT, preferred_element_type=F32)


def row8(ref, row):
    return ref[pl.ds(row, 8, stride=0), :]


def row16(ref, row):
    return jnp.concatenate([row8(ref, row)] * 2, 0).astype(BF16)


def high_low(x):
    high = x.astype(BF16)
    return high, (x - high.astype(F32)).astype(BF16)


def pack_virtual(offset, counts, data, cells, lines):
    lane = lax.broadcasted_iota(I32, (1, 512), 1)
    high = data[0, offset].astype(F32)
    cell = cells[offset]
    values = [
        jnp.where(lane < counts[0, offset], high[0:1], 0.0),
        high[1:2],
        high[2:3],
        high[3:4],
        (cell >> 8).astype(F32),
        (cell & 255).astype(F32),
    ]
    for field, value in enumerate(values):
        for quarter in range(4):
            at = 4 * field + quarter
            lines[at : at + 1, :] = value[:, 128 * quarter : 128 * quarter + 128]
    lines[24:32, :] = jnp.zeros((8, 128), F32)
    return lines[...].astype(BF16)


def fine_kernel(offsets, split, counts, vcounts, data_hbm, cells_hbm, vdata, vcells, face, wait, *rest):
    outs, rest = rest[:split], rest[split:]
    data, cells, total, fields, places, lines, number, sems = rest
    patches = 16 * len(offsets)
    copies = []
    for at, offset in enumerate(offsets):
        copies.append(
            pltpu.make_async_copy(
                data_hbm.at[offset], data.at[pl.ds(16 * at, 16)], sems.at[2 * at]
            )
        )
        copies.append(
            pltpu.make_async_copy(
                cells_hbm.at[0, offset], cells.at[pl.ds(16 * at, 16)], sems.at[2 * at + 1]
            )
        )
    for copy in copies:
        copy.start()
    total[...] = jnp.zeros_like(total)
    work = jnp.int32(0)
    for at, offset in enumerate(offsets):
        for patch in range(16):
            live = counts[offset, 0, patch]
            number[16 * at + patch] = live
            work = work + jnp.maximum((live + (LANES - 1)) >> 8, 1)
    for extra in range(UNROLL + 4):
        number[patches + extra] = 0
    steps = lax.div(work + (UNROLL - 1), UNROLL)
    each = len(offsets) // split
    for index, offset in enumerate(offsets):
        slot = 17 * (index % each) + 16
        outs[index // each][slot] = pack_virtual(offset, vcounts, vdata, vcells, lines)
    if len(offsets) == 6:
        high, low = high_low(face[...])
        outs[1][51] = high[0:32]
        outs[1][52] = low[0:32]
        high, low = high_low(jnp.concatenate([face[32:40, :], jnp.zeros((8, 128), F32)], 0))
        outs[1][53] = jnp.concatenate([high, low], 0)
    lane = lax.broadcasted_iota(I32, (8, 128), 1)
    here = sublane(16, 128).astype(BF16)
    before = (sublane(16, 128) - 1.0).astype(BF16)
    rows = sublane(8, 128)
    zero = jnp.zeros((16, 128), BF16)
    for copy in copies:
        copy.wait()

    def deposit(unit, group, start, live, next_one, next_two):
        patch = jnp.minimum(group, patches - 1)
        at = pl.multiple_of(start, LANES)
        high = data[patch, start >> 8].astype(F32)
        cell = cells[pl.ds(patch, 1), pl.ds(at, LANES)]
        f = fields.at[unit]
        g = places.at[unit]
        f[0:8, :] = high
        f[8:16, :] = 1.0 - high
        g[0:1, :] = (cell >> 8).astype(F32)
        g[1:2, :] = (cell & 15).astype(F32)
        g[2:3, :] = ((cell >> 4) & 3).astype(F32)
        g[3:4, :] = ((cell >> 6) & 3).astype(F32)
        left, right = [], []
        for half in range(2):
            wide = slice(128 * half, 128 * half + 128)

            def up(field, half=half):
                return row8(f, 4 * half + field)

            def down(field, half=half):
                return row8(f, 8 + 4 * half + field)

            def double(x):
                return jnp.concatenate([x, x], 0).astype(BF16)

            def where_at(field, wide=wide):
                return g[pl.ds(field, 8, stride=0), :][:, wide]

            mass = jnp.where(lane < live - 128 * half, up(0), 0.0)
            c0, c1 = double(down(3) * mass), double(up(3) * mass)
            x0, x1 = double(down(1)), double(up(1))
            inner = where_at(2)
            f[16 + 8 * half : 24 + 8 * half, :] = jnp.where(
                rows == inner, down(2), jnp.where(rows - 1.0 == inner, up(2), 0.0)
            )
            x, z, outer = double(where_at(0)), double(where_at(1)), double(where_at(3))
            along_x = jnp.where(here == x, x0, jnp.where(before == x, x1, zero))
            along_z = jnp.where(here == z, c0, jnp.where(before == z, c1, zero))
            left.append(
                jnp.concatenate(
                    [jnp.where(outer == BF16(k), along_x, zero) for k in range(4)], 0
                )
            )
            right.append(
                jnp.concatenate(
                    [row16(f, 16 + 8 * half + k) * along_z for k in range(5)], 0
                )
            )
        total[patch, :, 0:80] += dot_nt(
            jnp.concatenate(left, 1), jnp.concatenate(right, 1)
        )
        last = live <= LANES
        group = jnp.where(last, group + 1, group)
        return (
            group,
            jnp.where(last, 0, start + LANES),
            jnp.where(last, next_one, live - LANES),
            jnp.where(last, next_two, next_one),
            number[group + 2],
        )

    def body(_, state):
        for unit in range(UNROLL):
            state = deposit(unit, *state)
        return state

    none = jnp.int32(0)
    lax.fori_loop(0, steps, body, (none, none, number[0], number[1], number[2]))
    lane = lax.broadcasted_iota(I32, (16, 128), 1)

    for index in range(split):
        out = outs[index]

        def fold(k, _, index=index, out=out):
            group = 16 * each * index + k
            for half in range(2):
                at = 32 * half
                even = total[group, at : at + 16]
                odd = total[group, at + 16 : at + 32]
                prior = total[group, at - 16 : at] if half else jnp.zeros((16, 128), F32)
                swapped = pltpu.roll(jnp.where(lane < 64, odd, prior), 64, 1)
                out[k + (k >> 4), 16 * half : 16 * half + 16] = (even + swapped).astype(BF16)
            return 0

        lax.fori_loop(0, 16 * each, fold, 0, unroll=8)


def fine_part(offsets, sizes, counts, vcounts, data, cells, vdata, vcells, face, wait):
    slots = cells.shape[3]
    patches = 16 * len(offsets)
    full = pl.BlockSpec(memory_space=pltpu.VMEM)
    smem = pl.BlockSpec(memory_space=pltpu.SMEM)
    anywhere = pl.BlockSpec(memory_space=pl.ANY)
    return pl.pallas_call(
        functools.partial(fine_kernel, offsets, len(sizes)),
        in_specs=[smem, smem, anywhere, anywhere, full, full, full, anywhere],
        out_specs=[full] * len(sizes),
        scratch_shapes=[
            pltpu.VMEM((patches, slots // LANES, 8, 128), BF16),
            pltpu.VMEM((patches, slots), I32),
            pltpu.VMEM((patches, 64, 128), F32),
            pltpu.VMEM((UNROLL, 32, 128), F32),
            pltpu.VMEM((UNROLL, 8, LANES), F32),
            pltpu.VMEM((32, 128), F32),
            pltpu.SMEM((patches + UNROLL + 4,), I32),
            pltpu.SemaphoreType.DMA((2 * len(offsets),)),
        ],
        out_shape=[jax.ShapeDtypeStruct((size, 32, 128), BF16) for size in sizes],
        compiler_params=pltpu.CompilerParams(vmem_limit_bytes=VMEM_LIMIT),
        cost_estimate=pl.CostEstimate(
            flops=4 * patches * slots * 64 * 128, bytes_accessed=40000 * patches, transcendentals=0
        ),
        name="fine",
    )(counts, vcounts, data, cells, vdata, vcells, face, wait)


def tile_kernel(counts, data, cells, core, face_x, face_y, grid, fields):
    grid[...] = jnp.zeros_like(grid)
    lane = lax.broadcasted_iota(I32, (1, 128), 1)
    here = sublane(16, LANES).astype(BF16)
    before = (sublane(16, LANES) - 1.0).astype(BF16)
    fifteen = (sublane(16, LANES) + 15.0).astype(BF16)
    rows = sublane(16, LANES)
    zero = jnp.zeros((16, LANES), BF16)

    def column(col, _):
        tx = col >> 2
        ty = col & 3
        acc = jnp.zeros((144, 128), F32)
        for pair in range(8):
            tz = 2 * pair
            f = fields.at[pair]
            high = jnp.concatenate(
                [data[tx, ty, tz].astype(F32), data[tx, ty, tz + 1].astype(F32)], 1
            )
            low = 1.0 - high
            live = jnp.concatenate(
                [jnp.where(lane < counts[tx, ty, tz], 1.0, 0.0),
                 jnp.where(lane < counts[tx, ty, tz + 1], 1.0, 0.0)], 1
            )
            cell = jnp.concatenate(
                [cells[tx, ty, tz : tz + 1, :], cells[tx, ty, tz + 1 : tz + 2, :] + 1024], 1
            )
            mass = high[0:1] * live
            f[0:4, :] = high
            f[4:8, :] = low
            f[8:9, :] = high[3:4] * mass
            f[9:10, :] = low[3:4] * mass
            f[10:11, :] = ((cell >> 6) & 7).astype(F32)
            f[11:12, :] = ((cell >> 3) & 7).astype(F32)
            f[12:13, :] = ((cell & 7) + ((cell >> 10) << 3)).astype(F32)
            x = jnp.concatenate([row8(f, 10)] * 2, 0)
            low_x = jnp.concatenate([row8(f, 5)] * 2, 0)
            high_x = jnp.concatenate([row8(f, 1)] * 2, 0)
            f[16:32, :] = jnp.where(
                rows == x, low_x, jnp.where(rows - 1.0 == x, high_x, 0.0)
            )
            y, z = row16(f, 11), row16(f, 12)
            c0, c1 = row16(f, 9), row16(f, 8)
            along_y = jnp.where(
                here == y, row16(f, 6), jnp.where(before == y, row16(f, 2), zero)
            )
            along_z = jnp.concatenate(
                [jnp.where(here == z, c0, jnp.where(before == z, c1, zero)),
                 jnp.where(fifteen == z, c1, zero)], 0
            )
            left = jnp.concatenate([row16(f, 16 + k) * along_y for k in range(9)], 0)
            part = jnp.concatenate(
                [dot_nt(left, along_z), jnp.zeros((144, 96), F32)], 1
            )
            acc = acc + (pltpu.roll(part, 16 * pair, 1) if pair else part)
        for k in range(9):
            grid[8 * tx + k, pl.ds(pl.multiple_of(8 * ty, 8), 16), :] += acc[
                16 * k : 16 * k + 16
            ]
        return 0

    lax.fori_loop(0, 8, column, 0)
    core[...] = grid[0:16, 0:32, :]
    face_x[...] = grid[16]
    face_y[...] = grid[0:16, 32, :]


def tile_part(counts, data, cells):
    full = pl.BlockSpec(memory_space=pltpu.VMEM)
    smem = pl.BlockSpec(memory_space=pltpu.SMEM)
    return pl.pallas_call(
        tile_kernel,
        in_specs=[smem, full, full],
        out_specs=[full] * 3,
        out_shape=[
            jax.ShapeDtypeStruct((16, 32, 128), F32),
            jax.ShapeDtypeStruct((40, 128), F32),
            jax.ShapeDtypeStruct((16, 128), F32),
        ],
        scratch_shapes=[
            pltpu.VMEM((17, 40, 128), F32),
            pltpu.VMEM((8, 32, LANES), F32),
        ],
        compiler_params=pltpu.CompilerParams(vmem_limit_bytes=VMEM_LIMIT),
        name="tiles",
    )(counts, data, cells)


def virtual_deposit(packs, out, lines, fields):
    lanes = 512
    rows = sublane(16, lanes)
    zero = jnp.zeros((16, lanes), BF16)

    def place(at):
        return (rows + float(at)).astype(BF16)

    for which, (source, slot) in enumerate(packs):
        f = fields.at[which & 1]
        g = lines.at[which & 1]
        g[...] = source[slot].astype(F32)

        def value(field):
            return jnp.concatenate(
                [g[4 * field + quarter : 4 * field + quarter + 1, :] for quarter in range(4)], 1
            )

        cell = (value(4) * 256.0 + value(5)).astype(I32)
        mass, fx, fy, fz = value(0), value(1), value(2), value(3)
        f[0:1, :] = fx
        f[1:2, :] = 1.0 - fx
        f[2:3, :] = fy
        f[3:4, :] = 1.0 - fy
        f[4:5, :] = fz * mass
        f[5:6, :] = (1.0 - fz) * mass
        f[10:11, :] = (cell >> 12).astype(F32)
        f[11:12, :] = ((cell >> 7) & 31).astype(F32)
        f[12:13, :] = (cell & 127).astype(F32)
        f[13:14, :] = ((cell + 1) & 127).astype(F32)
        x = jnp.concatenate([row8(f, 10)] * 2, 0)
        low_x = jnp.concatenate([row8(f, 1)] * 2, 0)
        high_x = jnp.concatenate([row8(f, 0)] * 2, 0)
        f[16:32, :] = jnp.where(
            rows == x, low_x, jnp.where(rows - 1.0 == x, high_x, 0.0)
        )
        y, z, z_next = row16(f, 11), row16(f, 12), row16(f, 13)
        c0, c1 = row16(f, 5), row16(f, 4)
        y0, y1 = row16(f, 3), row16(f, 2)
        along_y = [
            jnp.where(place(16 * h) == y, y0, jnp.where(place(16 * h - 1) == y, y1, zero))
            for h in range(2)
        ]
        along_z = jnp.concatenate(
            [
                jnp.where(
                    place(16 * k) == z, c0, jnp.where(place(16 * k) == z_next, c1, zero)
                )
                for k in range(8)
            ],
            0,
        )
        left = []
        for k in range(16):
            w = row16(f, 16 + k)
            left += [w * along_y[0], w * along_y[1]]
        out[...] += dot_nt(jnp.concatenate(left, 0), along_z)


def base_kernel(own, right, left, core, out, lines, fields):
    out[...] = core[...].reshape(512, 128)
    out[0:32, :] += left[51].astype(F32) + left[52].astype(F32)
    virtual_deposit([(own, 16), (right, 33), (left, 33)], out, lines, fields)


def base_part(*args):
    full = pl.BlockSpec(memory_space=pltpu.VMEM)
    return pl.pallas_call(
        base_kernel,
        in_specs=[full] * 4,
        out_specs=full,
        out_shape=jax.ShapeDtypeStruct((512, 128), F32),
        scratch_shapes=[pltpu.VMEM((2, 32, 128), F32), pltpu.VMEM((2, 32, 512), F32)],
        compiler_params=pltpu.CompilerParams(vmem_limit_bytes=SMALL_LIMIT),
        cost_estimate=pl.CostEstimate(
            flops=6 * 3 * 512 * 512 * 128, bytes_accessed=1000000, transcendentals=0
        ),
        name="base",
    )(*args)


def join_kernel(own, right, left, face_y, up, down):
    for at, (out, slot) in enumerate(((up, 0), (down, 34))):
        for patch in range(16):
            out[patch] = (
                own[17 * at + patch].astype(F32)
                + right[slot + patch].astype(F32)
                + left[slot + patch].astype(F32)
            ).astype(BF16)
        out[16] = own[17 * at + 16]
        out[17] = right[slot + 16]
        out[18] = left[slot + 16]
    corner = left[53].astype(F32)
    row = lax.broadcasted_iota(I32, (16, 128), 0)
    face = face_y[...] + jnp.where(row == 0, corner[0:16] + corner[16:32], 0.0)
    high, low = high_low(face)
    down[19] = jnp.concatenate([high, low], 0)


def join_part(*args):
    full = pl.BlockSpec(memory_space=pltpu.VMEM)
    return pl.pallas_call(
        join_kernel,
        in_specs=[full] * 4,
        out_specs=[full] * 2,
        out_shape=[jax.ShapeDtypeStruct((size, 32, 128), BF16) for size in (19, 20)],
        compiler_params=pltpu.CompilerParams(vmem_limit_bytes=SMALL_LIMIT),
        name="join",
    )(*args)


def last_kernel(part, own, right, left, up, down, base, out, patches, fields, lines):
    for patch in range(16):
        mass = (
            (own[patch].astype(F32) + left[17 + patch].astype(F32))
            + (right[17 + patch].astype(F32) + up[patch].astype(F32))
        ) + down[patch].astype(F32)
        patches[32 * patch : 32 * patch + 32, :] = mass
    for group in range(2):
        for half in range(2):
            for x in range(16):
                block = patches[pl.ds(256 * group + 16 * half + x, 8, stride=32), :]
                at = 128 * (2 * x + half)
                out[8 * group : 8 * group + 8, at : at + 128] = block
    base[...] = part[...]
    both = down[19].astype(F32)
    face = both[0:16] + both[16:32]
    for x in range(16):
        base[32 * x : 32 * x + 1, :] += face[x : x + 1, :]
    virtual_deposit(
        [(source, slot) for source in (up, down) for slot in (16, 17, 18)], base, lines, fields
    )


def last_part(*args):
    full = pl.BlockSpec(memory_space=pltpu.VMEM)
    return pl.pallas_call(
        last_kernel,
        in_specs=[full] * 6,
        out_specs=[full] * 2,
        out_shape=[
            jax.ShapeDtypeStruct((512, 128), F32),
            jax.ShapeDtypeStruct((16, 4096), F32),
        ],
        scratch_shapes=[
            pltpu.VMEM((512, 128), F32),
            pltpu.VMEM((2, 32, 512), F32),
            pltpu.VMEM((2, 32, 128), F32),
        ],
        compiler_params=pltpu.CompilerParams(vmem_limit_bytes=SMALL_LIMIT),
        name="last",
    )(*args)


def on_device(
    part_data,
    tile_cells,
    tile_counts,
    ghost_data,
    halo_refined_cells,
    ghost_counts,
    virt_data,
    virt_cells,
    phantom_slot_counts,
):
    core, face_x, face_y = tile_part(tile_counts, part_data, tile_cells)
    sources, own_patches, fields, slots = ghost_data.shape[1:]
    tiled = ghost_data.reshape(sources, own_patches, fields, slots // LANES, 2, 128)
    tiled = tiled.transpose(0, 1, 3, 4, 2, 5)
    tiled = tiled.reshape(sources, own_patches, slots // LANES, 8, 128)
    counts = jnp.swapaxes(ghost_counts, 0, 1)
    ghosts = (counts, phantom_slot_counts, tiled, halo_refined_cells)
    ghosts += (virt_data, jnp.swapaxes(virt_cells, 0, 1), face_x)
    toward, away = fine_part((0, 1, 2, 6, 7, 8), (51, 54), *ghosts, core)
    right = shift(toward, "gx", -1)
    left = shift(away, "gx", 1)
    (sides,) = fine_part((3, 5), (34,), *ghosts, away)
    up, down = join_part(sides, right, left, face_y)
    from_up = shift(up, "gy", -1)
    from_down = shift(down, "gy", 1)
    (own,) = fine_part((4,), (17,), *ghosts, down)
    part = base_part(own, right, left, core)
    base, fine_mass = last_part(part, own, right, left, from_up, from_down)
    return base.reshape(16, 32, 128), fine_mass


def solution(mesh):
    return jax.shard_map(
        on_device,
        mesh=mesh,
        in_specs=(
            P("gx", "gy", None, None, None),
            P("gx", "gy", None, None),
            P("gx", "gy", None),
            P(("gx", "gy"), None, None, None, None),
            P(("gx", "gy"), None, None, None),
            P(("gx", "gy"), None, None),
            P(("gx", "gy"), None, None, None),
            P(("gx", "gy"), None, None),
            P(("gx", "gy"), None),
        ),
        out_specs=(P("gx", "gy", None), P(("gx", "gy"), None)),
        check_vma=False,
    )
```

```python
import functools

import jax
import jax.numpy as jnp
from jax import lax
from jax.experimental import pallas as pl
from jax.experimental.pallas import tpu as pltpu
from jax.sharding import PartitionSpec as P

BF16 = jnp.bfloat16
F32 = jnp.float32
I32 = jnp.int32
NT = (((1,), (1,)), ((), ()))
LANES = 256
OUTER = (0, 1, 2, 6, 7, 8)
VMEM_LIMIT = 16 * 2**20
FIRST_LIMIT = 56 * 2**20


def shift(x, axis, by):
    devices = lax.axis_size(axis)
    return lax.ppermute(x, axis, [(i, (i + by) % devices) for i in range(devices)])


def sublane(rows, lanes):
    return lax.broadcasted_iota(I32, (rows, lanes), 0).astype(F32)


def dot_nt(a, b):
    return lax.dot_general(a, b, NT, preferred_element_type=F32)


def row8(ref, row):
    return ref[pl.ds(row, 8, stride=0), :]


def row16(ref, row):
    return jnp.concatenate([row8(ref, row)] * 2, 0).astype(BF16)


def high_low(x):
    high = x.astype(BF16)
    return high, (x - high.astype(F32)).astype(BF16)


def pack_virtual(offset, counts, data, cells, lines):
    lane = lax.broadcasted_iota(I32, (1, 512), 1)
    high = data[0, offset].astype(F32)
    cell = cells[offset]
    values = [
        jnp.where(lane < counts[0, offset], high[0:1], 0.0),
        high[1:2],
        high[2:3],
        high[3:4],
        (cell >> 8).astype(F32),
        (cell & 255).astype(F32),
    ]
    for field, value in enumerate(values):
        for quarter in range(4):
            at = 4 * field + quarter
            lines[at : at + 1, :] = value[:, 128 * quarter : 128 * quarter + 128]
    lines[24:32, :] = jnp.zeros((8, 128), F32)
    return lines[...].astype(BF16)


def deposit_ghosts(offsets, unroll, counts, get_data, get_cells, outs, total, fields, places, number, ready):
    split = len(outs)
    patches = 16 * len(offsets)
    each = len(offsets) // split
    total[...] = jnp.zeros_like(total)
    work = jnp.int32(0)
    for at, offset in enumerate(offsets):
        for patch in range(16):
            live = counts[offset, 0, patch]
            number[16 * at + patch] = live
            work = work + jnp.maximum((live + (LANES - 1)) >> 8, 1)
    for extra in range(unroll + 4):
        number[patches + extra] = 0
    steps = lax.div(work + (unroll - 1), unroll)
    lane = lax.broadcasted_iota(I32, (8, 128), 1)
    here = sublane(16, 128).astype(BF16)
    before = (sublane(16, 128) - 1.0).astype(BF16)
    rows = sublane(8, 128)
    zero = jnp.zeros((16, 128), BF16)
    for copy in ready:
        copy.wait()

    def deposit(unit, group, start, live, next_one, next_two):
        patch = jnp.minimum(group, patches - 1)
        at = pl.multiple_of(start, LANES)
        high = get_data(patch, start >> 8).astype(F32)
        cell = get_cells(patch, at)
        f = fields.at[unit]
        g = places.at[unit]
        f[0:8, :] = high
        f[8:16, :] = 1.0 - high
        g[0:1, :] = (cell >> 8).astype(F32)
        g[1:2, :] = (cell & 15).astype(F32)
        g[2:3, :] = ((cell >> 4) & 3).astype(F32)
        g[3:4, :] = ((cell >> 6) & 3).astype(F32)
        left, right = [], []
        for half in range(2):
            wide = slice(128 * half, 128 * half + 128)

            def up(field, half=half):
                return row8(f, 4 * half + field)

            def down(field, half=half):
                return row8(f, 8 + 4 * half + field)

            def double(x):
                return jnp.concatenate([x, x], 0).astype(BF16)

            def where_at(field, wide=wide):
                return g[pl.ds(field, 8, stride=0), :][:, wide]

            mass = jnp.where(lane < live - 128 * half, up(0), 0.0)
            c0, c1 = double(down(3) * mass), double(up(3) * mass)
            x0, x1 = double(down(1)), double(up(1))
            inner = where_at(2)
            f[16 + 8 * half : 24 + 8 * half, :] = jnp.where(
                rows == inner, down(2), jnp.where(rows - 1.0 == inner, up(2), 0.0)
            )
            x, z, outer = double(where_at(0)), double(where_at(1)), double(where_at(3))
            along_x = jnp.where(here == x, x0, jnp.where(before == x, x1, zero))
            along_z = jnp.where(here == z, c0, jnp.where(before == z, c1, zero))
            left.append(
                jnp.concatenate(
                    [jnp.where(outer == BF16(k), along_x, zero) for k in range(4)], 0
                )
            )
            right.append(
                jnp.concatenate(
                    [row16(f, 16 + 8 * half + k) * along_z for k in range(5)], 0
                )
            )
        total[patch, :, 0:80] += dot_nt(
            jnp.concatenate(left, 1), jnp.concatenate(right, 1)
        )
        last = live <= LANES
        group = jnp.where(last, group + 1, group)
        return (
            group,
            jnp.where(last, 0, start + LANES),
            jnp.where(last, next_one, live - LANES),
            jnp.where(last, next_two, next_one),
            number[group + 2],
        )

    def body(_, state):
        for unit in range(unroll):
            state = deposit(unit, *state)
        return state

    none = jnp.int32(0)
    lax.fori_loop(0, steps, body, (none, none, number[0], number[1], number[2]))
    lane = lax.broadcasted_iota(I32, (16, 128), 1)

    for index in range(split):
        out = outs[index]

        def fold(k, _, index=index, out=out):
            group = 16 * each * index + k
            for half in range(2):
                at = 32 * half
                even = total[group, at : at + 16]
                odd = total[group, at + 16 : at + 32]
                prior = total[group, at - 16 : at] if half else jnp.zeros((16, 128), F32)
                swapped = pltpu.roll(jnp.where(lane < 64, odd, prior), 64, 1)
                out[k + (k >> 4) if split > 1 else k, 16 * half : 16 * half + 16] = (even + swapped).astype(BF16)
            return 0

        lax.fori_loop(0, 16 * each, fold, 0, unroll=8)


def deposit_tiles(counts, data, cells, core, face_y, grid, fields):
    lane = lax.broadcasted_iota(I32, (1, 128), 1)
    here = sublane(16, LANES).astype(BF16)
    before = (sublane(16, LANES) - 1.0).astype(BF16)
    fifteen = (sublane(16, LANES) + 15.0).astype(BF16)
    rows = sublane(16, LANES)
    zero = jnp.zeros((16, LANES), BF16)

    def column(col, _):
        tx = col >> 2
        ty = col & 3
        acc = jnp.zeros((144, 128), F32)
        for pair in range(8):
            tz = 2 * pair
            f = fields.at[pair]
            high = jnp.concatenate(
                [data[tx, ty, tz].astype(F32), data[tx, ty, tz + 1].astype(F32)], 1
            )
            low = 1.0 - high
            live = jnp.concatenate(
                [jnp.where(lane < counts[tx, ty, tz], 1.0, 0.0),
                 jnp.where(lane < counts[tx, ty, tz + 1], 1.0, 0.0)], 1
            )
            cell = jnp.concatenate(
                [cells[tx, ty, tz : tz + 1, :], cells[tx, ty, tz + 1 : tz + 2, :] + 1024], 1
            )
            mass = high[0:1] * live
            f[0:4, :] = high
            f[4:8, :] = low
            f[8:9, :] = high[3:4] * mass
            f[9:10, :] = low[3:4] * mass
            f[10:11, :] = ((cell >> 6) & 7).astype(F32)
            f[11:12, :] = ((cell >> 3) & 7).astype(F32)
            f[12:13, :] = ((cell & 7) + ((cell >> 10) << 3)).astype(F32)
            x = jnp.concatenate([row8(f, 10)] * 2, 0)
            low_x = jnp.concatenate([row8(f, 5)] * 2, 0)
            high_x = jnp.concatenate([row8(f, 1)] * 2, 0)
            f[16:32, :] = jnp.where(
                rows == x, low_x, jnp.where(rows - 1.0 == x, high_x, 0.0)
            )
            y, z = row16(f, 11), row16(f, 12)
            c0, c1 = row16(f, 9), row16(f, 8)
            along_y = jnp.where(
                here == y, row16(f, 6), jnp.where(before == y, row16(f, 2), zero)
            )
            along_z = jnp.concatenate(
                [jnp.where(here == z, c0, jnp.where(before == z, c1, zero)),
                 jnp.where(fifteen == z, c1, zero)], 0
            )
            left = jnp.concatenate([row16(f, 16 + k) * along_y for k in range(9)], 0)
            part = jnp.concatenate(
                [dot_nt(left, along_z), jnp.zeros((144, 96), F32)], 1
            )
            acc = acc + (pltpu.roll(part, 16 * pair, 1) if pair else part)
        for k in range(9):
            grid[8 * tx + k, pl.ds(pl.multiple_of(8 * ty, 8), 16), :] += acc[
                16 * k : 16 * k + 16
            ]
        return 0

    lax.fori_loop(0, 8, column, 0)
    core[...] = grid[0:16, 0:32, :]
    face_y[...] = grid[0:16, 32, :]


def first_kernel(
    counts, vcounts, tcounts, data_hbm, cells_hbm, vdata_hbm, vcells_hbm, tdata_hbm, tcells_hbm,
    toward, away, packs, core, face_y,
    data, cells, vdata, vcells, tdata, tcells, grid, tile_fields, total, fields, places, lines, number, sems,
):
    sources = [(tdata_hbm, tdata), (tcells_hbm, tcells), (vdata_hbm, vdata), (vcells_hbm, vcells)]
    for at, offset in enumerate(OUTER):
        here = pl.ds(16 * at, 16)
        sources.append((data_hbm.at[offset], data.at[here]))
        sources.append((cells_hbm.at[0, offset], cells.at[here]))
    copies = [
        pltpu.make_async_copy(source, target, sems.at[index])
        for index, (source, target) in enumerate(sources)
    ]
    for copy in copies:
        copy.start()
    grid[...] = jnp.zeros_like(grid)
    for copy in copies[:2]:
        copy.wait()
    deposit_tiles(tcounts, tdata, tcells, core, face_y, grid, tile_fields)
    for copy in copies[2:4]:
        copy.wait()
    for offset in range(9):
        out = (toward, packs, away)[offset // 3]
        slot = offset % 3 if out is packs else 17 * (offset % 3) + 16
        out[slot] = pack_virtual(offset, vcounts, vdata, vcells, lines)
    high, low = high_low(grid[16, 0:32, :])
    away[51] = high
    away[52] = low
    high, low = high_low(
        jnp.concatenate([grid[16, 32:40, :], jnp.zeros((8, 128), F32)], 0)
    )
    away[53] = jnp.concatenate([high, low], 0)
    deposit_ghosts(
        OUTER,
        32,
        counts,
        lambda group, chunk: data[group, chunk],
        lambda group, at: cells[pl.ds(group, 1), pl.ds(at, LANES)],
        (toward, away),
        total,
        fields,
        places,
        number,
        copies[4:],
    )


def first_part(counts, vcounts, tcounts, data, cells, vdata, vcells, tdata, tcells):
    slots = cells.shape[3]
    patches = 16 * len(OUTER)
    full = pl.BlockSpec(memory_space=pltpu.VMEM)
    smem = pl.BlockSpec(memory_space=pltpu.SMEM)
    hbm = pl.BlockSpec(memory_space=pltpu.HBM)
    return pl.pallas_call(
        first_kernel,
        in_specs=[smem] * 3 + [hbm] * 6,
        out_specs=[full] * 5,
        scratch_shapes=[
            pltpu.VMEM((patches, slots // LANES, 8, 128), BF16),
            pltpu.VMEM((patches, slots), I32),
            pltpu.VMEM(vdata.shape, BF16),
            pltpu.VMEM(vcells.shape, I32),
            pltpu.VMEM(tdata.shape, BF16),
            pltpu.VMEM(tcells.shape, I32),
            pltpu.VMEM((17, 40, 128), F32),
            pltpu.VMEM((8, 32, LANES), F32),
            pltpu.VMEM((patches, 64, 128), F32),
            pltpu.VMEM((32, 32, 128), F32),
            pltpu.VMEM((32, 8, LANES), F32),
            pltpu.VMEM((32, 128), F32),
            pltpu.SMEM((patches + 36,), I32),
            pltpu.SemaphoreType.DMA((16,)),
        ],
        out_shape=[
            jax.ShapeDtypeStruct((51, 32, 128), BF16),
            jax.ShapeDtypeStruct((54, 32, 128), BF16),
            jax.ShapeDtypeStruct((3, 32, 128), BF16),
            jax.ShapeDtypeStruct((16, 32, 128), F32),
            jax.ShapeDtypeStruct((16, 128), F32),
        ],
        compiler_params=pltpu.CompilerParams(vmem_limit_bytes=FIRST_LIMIT),
        cost_estimate=pl.CostEstimate(
            flops=4 * patches * slots * 64 * 128, bytes_accessed=4000000, transcendentals=0
        ),
        name="first",
    )(counts, vcounts, tcounts, data, cells, vdata, vcells, tdata, tcells)


def own_kernel(
    offsets, counts, data, cells, wait, out, total, fields, places, number
):
    def split(group):
        return offsets[0] + 2 * (group >> 4), group & 15

    def get_data(group, chunk):
        offset, patch = split(group)
        return data[offset, patch, chunk]

    def get_cells(group, at):
        offset, patch = split(group)
        return cells[0, offset, pl.ds(patch, 1), pl.ds(at, LANES)]

    deposit_ghosts(
        offsets, 24, counts, get_data, get_cells, (out,), total, fields, places, number, ()
    )


def own_part(offsets, counts, data, cells, wait):
    slots = cells.shape[3]
    patches = 16 * len(offsets)
    full = pl.BlockSpec(memory_space=pltpu.VMEM)
    smem = pl.BlockSpec(memory_space=pltpu.SMEM)
    anywhere = pl.BlockSpec(memory_space=pl.ANY)
    return pl.pallas_call(
        functools.partial(own_kernel, offsets),
        in_specs=[smem, full, full, anywhere],
        out_specs=full,
        scratch_shapes=[
            pltpu.VMEM((patches, 64, 128), F32),
            pltpu.VMEM((24, 32, 128), F32),
            pltpu.VMEM((24, 8, LANES), F32),
            pltpu.SMEM((patches + 28,), I32),
        ],
        out_shape=jax.ShapeDtypeStruct((patches, 32, 128), BF16),
        compiler_params=pltpu.CompilerParams(vmem_limit_bytes=VMEM_LIMIT),
        cost_estimate=pl.CostEstimate(
            flops=4 * patches * slots * 64 * 128, bytes_accessed=4000000, transcendentals=0
        ),
        name="own",
    )(counts, data, cells, wait)


def virtual_deposit(packs, out, lines, fields):
    lanes = 512
    rows = sublane(16, lanes)
    zero = jnp.zeros((16, lanes), BF16)

    def place(at):
        return (rows + float(at)).astype(BF16)

    for which, (source, slot) in enumerate(packs):
        f = fields.at[which & 1]
        g = lines.at[which & 1]
        g[...] = source[slot].astype(F32)

        def value(field):
            return jnp.concatenate(
                [g[4 * field + quarter : 4 * field + quarter + 1, :] for quarter in range(4)], 1
            )

        cell = (value(4) * 256.0 + value(5)).astype(I32)
        mass, fx, fy, fz = value(0), value(1), value(2), value(3)
        f[0:1, :] = fx
        f[1:2, :] = 1.0 - fx
        f[2:3, :] = fy
        f[3:4, :] = 1.0 - fy
        f[4:5, :] = fz * mass
        f[5:6, :] = (1.0 - fz) * mass
        f[10:11, :] = (cell >> 12).astype(F32)
        f[11:12, :] = ((cell >> 7) & 31).astype(F32)
        f[12:13, :] = (cell & 127).astype(F32)
        f[13:14, :] = ((cell + 1) & 127).astype(F32)
        x = jnp.concatenate([row8(f, 10)] * 2, 0)
        low_x = jnp.concatenate([row8(f, 1)] * 2, 0)
        high_x = jnp.concatenate([row8(f, 0)] * 2, 0)
        f[16:32, :] = jnp.where(
            rows == x, low_x, jnp.where(rows - 1.0 == x, high_x, 0.0)
        )
        y, z, z_next = row16(f, 11), row16(f, 12), row16(f, 13)
        c0, c1 = row16(f, 5), row16(f, 4)
        y0, y1 = row16(f, 3), row16(f, 2)
        along_y = [
            jnp.where(place(16 * h) == y, y0, jnp.where(place(16 * h - 1) == y, y1, zero))
            for h in range(2)
        ]
        along_z = jnp.concatenate(
            [
                jnp.where(
                    place(16 * k) == z, c0, jnp.where(place(16 * k) == z_next, c1, zero)
                )
                for k in range(8)
            ],
            0,
        )
        left = []
        for k in range(16):
            w = row16(f, 16 + k)
            left += [w * along_y[0], w * along_y[1]]
        out[...] += dot_nt(jnp.concatenate(left, 0), along_z)


def base_kernel(packs, right, left, core, out, lines, fields):
    out[...] = core[...].reshape(512, 128)
    out[0:32, :] += left[51].astype(F32) + left[52].astype(F32)
    virtual_deposit([(packs, 1), (right, 33), (left, 33)], out, lines, fields)


def base_part(*args):
    full = pl.BlockSpec(memory_space=pltpu.VMEM)
    return pl.pallas_call(
        base_kernel,
        in_specs=[full] * 4,
        out_specs=full,
        out_shape=jax.ShapeDtypeStruct((512, 128), F32),
        scratch_shapes=[pltpu.VMEM((2, 32, 128), F32), pltpu.VMEM((2, 32, 512), F32)],
        compiler_params=pltpu.CompilerParams(vmem_limit_bytes=VMEM_LIMIT),
        cost_estimate=pl.CostEstimate(
            flops=6 * 3 * 512 * 512 * 128, bytes_accessed=1000000, transcendentals=0
        ),
        name="base",
    )(*args)


def join_kernel(own, packs, right, left, face_y, up, down):
    for at, (out, slot) in enumerate(((up, 0), (down, 34))):
        for patch in range(16):
            out[patch] = (
                own[16 * at + patch].astype(F32)
                + right[slot + patch].astype(F32)
                + left[slot + patch].astype(F32)
            ).astype(BF16)
        out[16] = packs[2 * at]
        out[17] = right[slot + 16]
        out[18] = left[slot + 16]
    corner = left[53].astype(F32)
    row = lax.broadcasted_iota(I32, (16, 128), 0)
    face = face_y[...] + jnp.where(row == 0, corner[0:16] + corner[16:32], 0.0)
    high, low = high_low(face)
    down[19] = jnp.concatenate([high, low], 0)


def join_part(*args):
    full = pl.BlockSpec(memory_space=pltpu.VMEM)
    return pl.pallas_call(
        join_kernel,
        in_specs=[full] * 5,
        out_specs=[full] * 2,
        out_shape=[jax.ShapeDtypeStruct((size, 32, 128), BF16) for size in (19, 20)],
        compiler_params=pltpu.CompilerParams(vmem_limit_bytes=VMEM_LIMIT),
        name="join",
    )(*args)


def last_kernel(part, own, right, left, up, down, base, out, patches, fields, lines):
    for patch in range(16):
        mass = (
            (own[patch].astype(F32) + left[17 + patch].astype(F32))
            + (right[17 + patch].astype(F32) + up[patch].astype(F32))
        ) + down[patch].astype(F32)
        patches[32 * patch : 32 * patch + 32, :] = mass
    for group in range(2):
        for half in range(2):
            for x in range(16):
                block = patches[pl.ds(256 * group + 16 * half + x, 8, stride=32), :]
                at = 128 * (2 * x + half)
                out[8 * group : 8 * group + 8, at : at + 128] = block
    base[...] = part[...]
    both = down[19].astype(F32)
    face = both[0:16] + both[16:32]
    for x in range(16):
        base[32 * x : 32 * x + 1, :] += face[x : x + 1, :]
    virtual_deposit(
        [(source, slot) for source in (up, down) for slot in (16, 17, 18)], base, lines, fields
    )


def last_part(*args):
    full = pl.BlockSpec(memory_space=pltpu.VMEM)
    return pl.pallas_call(
        last_kernel,
        in_specs=[full] * 6,
        out_specs=[full] * 2,
        out_shape=[
            jax.ShapeDtypeStruct((512, 128), F32),
            jax.ShapeDtypeStruct((16, 4096), F32),
        ],
        scratch_shapes=[
            pltpu.VMEM((512, 128), F32),
            pltpu.VMEM((2, 32, 512), F32),
            pltpu.VMEM((2, 32, 128), F32),
        ],
        compiler_params=pltpu.CompilerParams(vmem_limit_bytes=VMEM_LIMIT),
        name="last",
    )(*args)


def on_device(
    part_data,
    tile_cells,
    tile_counts,
    ghost_data,
    halo_refined_cells,
    ghost_counts,
    virt_data,
    virt_cells,
    phantom_slot_counts,
):
    sources, own_patches, fields, slots = ghost_data.shape[1:]
    tiled = ghost_data.reshape(sources, own_patches, fields, slots // LANES, 2, 128)
    tiled = tiled.transpose(0, 1, 3, 4, 2, 5)
    tiled = tiled.reshape(sources, own_patches, slots // LANES, 8, 128)
    counts = jnp.swapaxes(ghost_counts, 0, 1)
    toward, away, packs, core, face_y = first_part(
        counts,
        phantom_slot_counts,
        tile_counts,
        tiled,
        halo_refined_cells,
        virt_data,
        jnp.swapaxes(virt_cells, 0, 1),
        part_data,
        tile_cells,
    )
    right = shift(toward, "gx", -1)
    left = shift(away, "gx", 1)
    sides = own_part((3, 5), counts, tiled, halo_refined_cells, away)
    up, down = join_part(sides, packs, right, left, face_y)
    from_up = shift(up, "gy", -1)
    from_down = shift(down, "gy", 1)
    own = own_part((4,), counts, tiled, halo_refined_cells, down)
    part = base_part(packs, right, left, core)
    base, fine_mass = last_part(part, own, right, left, from_up, from_down)
    return base.reshape(16, 32, 128), fine_mass


def solution(mesh):
    return jax.shard_map(
        on_device,
        mesh=mesh,
        in_specs=(
            P("gx", "gy", None, None, None),
            P("gx", "gy", None, None),
            P("gx", "gy", None),
            P(("gx", "gy"), None, None, None, None),
            P(("gx", "gy"), None, None, None),
            P(("gx", "gy"), None, None),
            P(("gx", "gy"), None, None, None),
            P(("gx", "gy"), None, None),
            P(("gx", "gy"), None),
        ),
        out_specs=(P("gx", "gy", None), P(("gx", "gy"), None)),
        check_vma=False,
    )
```

```python
import functools

import jax
import jax.numpy as jnp
from jax import lax
from jax.experimental import pallas as pl
from jax.experimental.pallas import tpu as pltpu
from jax.sharding import PartitionSpec as P

BF16 = jnp.bfloat16
F32 = jnp.float32
I32 = jnp.int32
NT = (((1,), (1,)), ((), ()))
LANES = 256
OUTER = (0, 1, 2, 6, 7, 8)
VMEM_LIMIT = 16 * 2**20
FIRST_LIMIT = 56 * 2**20


def shift(x, axis, by):
    devices = lax.axis_size(axis)
    return lax.ppermute(x, axis, [(i, (i + by) % devices) for i in range(devices)])


def sublane(rows, lanes):
    return lax.broadcasted_iota(I32, (rows, lanes), 0).astype(F32)


def dot_nt(a, b):
    return lax.dot_general(a, b, NT, preferred_element_type=F32)


def row8(ref, row):
    return ref[pl.ds(row, 8, stride=0), :]


def row16(ref, row):
    return jnp.concatenate([row8(ref, row)] * 2, 0).astype(BF16)


def high_low(x):
    high = x.astype(BF16)
    return high, (x - high.astype(F32)).astype(BF16)


def pack_virtual(offset, counts, data, cells, lines):
    lane = lax.broadcasted_iota(I32, (1, 512), 1)
    high = data[0, offset].astype(F32)
    cell = cells[offset]
    values = [
        jnp.where(lane < counts[0, offset], high[0:1], 0.0),
        high[1:2],
        high[2:3],
        high[3:4],
        (cell >> 8).astype(F32),
        (cell & 255).astype(F32),
    ]
    for field, value in enumerate(values):
        for quarter in range(4):
            at = 4 * field + quarter
            lines[at : at + 1, :] = value[:, 128 * quarter : 128 * quarter + 128]
    lines[24:32, :] = jnp.zeros((8, 128), F32)
    return lines[...].astype(BF16)


def deposit_ghosts(offsets, unroll, counts, get_data, get_cells, outs, total, fields, places, number, ready):
    split = len(outs)
    patches = 16 * len(offsets)
    each = len(offsets) // split
    total[...] = jnp.zeros_like(total)
    work = jnp.int32(0)
    for at, offset in enumerate(offsets):
        for patch in range(16):
            live = counts[offset, 0, patch]
            number[16 * at + patch] = live
            work = work + jnp.maximum((live + (LANES - 1)) >> 8, 1)
    for extra in range(unroll + 4):
        number[patches + extra] = 0
    steps = lax.div(work + (unroll - 1), unroll)
    lane = lax.broadcasted_iota(I32, (8, 128), 1)
    here = sublane(16, 128).astype(BF16)
    before = (sublane(16, 128) - 1.0).astype(BF16)
    rows = sublane(8, 128)
    zero = jnp.zeros((16, 128), BF16)
    for copy in ready:
        copy.wait()

    def deposit(unit, group, start, live, next_one, next_two):
        patch = jnp.minimum(group, patches - 1)
        at = pl.multiple_of(start, LANES)
        high = get_data(patch, start >> 8).astype(F32)
        cell = get_cells(patch, at)
        f = fields.at[unit]
        g = places.at[unit]
        f[0:8, :] = high
        f[8:16, :] = 1.0 - high
        g[0:1, :] = (cell >> 8).astype(F32)
        g[1:2, :] = (cell & 15).astype(F32)
        g[2:3, :] = ((cell >> 4) & 3).astype(F32)
        g[3:4, :] = ((cell >> 6) & 3).astype(F32)
        left, right = [], []
        for half in range(2):
            wide = slice(128 * half, 128 * half + 128)

            def up(field, half=half):
                return row8(f, 4 * half + field)

            def down(field, half=half):
                return row8(f, 8 + 4 * half + field)

            def double(x):
                return jnp.concatenate([x, x], 0).astype(BF16)

            def where_at(field, wide=wide):
                return g[pl.ds(field, 8, stride=0), :][:, wide]

            mass = jnp.where(lane < live - 128 * half, up(0), 0.0)
            c0, c1 = double(down(3) * mass), double(up(3) * mass)
            x0, x1 = double(down(1)), double(up(1))
            inner = where_at(2)
            f[16 + 8 * half : 24 + 8 * half, :] = jnp.where(
                rows == inner, down(2), jnp.where(rows - 1.0 == inner, up(2), 0.0)
            )
            x, z, outer = double(where_at(0)), double(where_at(1)), double(where_at(3))
            along_x = jnp.where(here == x, x0, jnp.where(before == x, x1, zero))
            along_z = jnp.where(here == z, c0, jnp.where(before == z, c1, zero))
            left.append(
                jnp.concatenate(
                    [jnp.where(outer == BF16(k), along_x, zero) for k in range(4)], 0
                )
            )
            right.append(
                jnp.concatenate(
                    [row16(f, 16 + 8 * half + k) * along_z for k in range(5)], 0
                )
            )
        total[patch, :, 0:80] += dot_nt(
            jnp.concatenate(left, 1), jnp.concatenate(right, 1)
        )
        last = live <= LANES
        group = jnp.where(last, group + 1, group)
        return (
            group,
            jnp.where(last, 0, start + LANES),
            jnp.where(last, next_one, live - LANES),
            jnp.where(last, next_two, next_one),
            number[group + 2],
        )

    def body(_, state):
        for unit in range(unroll):
            state = deposit(unit, *state)
        return state

    none = jnp.int32(0)
    lax.fori_loop(0, steps, body, (none, none, number[0], number[1], number[2]))
    lane = lax.broadcasted_iota(I32, (16, 128), 1)

    for index in range(split):
        out = outs[index]

        def fold(k, _, index=index, out=out):
            group = 16 * each * index + k
            for half in range(2):
                at = 32 * half
                even = total[group, at : at + 16]
                odd = total[group, at + 16 : at + 32]
                prior = total[group, at - 16 : at] if half else jnp.zeros((16, 128), F32)
                swapped = pltpu.roll(jnp.where(lane < 64, odd, prior), 64, 1)
                out[k + (k >> 4) if split > 1 else k, 16 * half : 16 * half + 16] = (even + swapped).astype(BF16)
            return 0

        lax.fori_loop(0, 16 * each, fold, 0, unroll=8)


def deposit_tiles(columns, counts, data, cells, grid, fields, places, depth):
    lane = lax.broadcasted_iota(I32, (8, 128), 1)
    here = sublane(16, 128).astype(BF16)
    before = (sublane(16, 128) - 1.0).astype(BF16)
    fifteen = (sublane(16, 128) + 15.0).astype(BF16)
    rows = sublane(16, 128)
    odd = lax.broadcasted_iota(I32, (2, 128), 0) * 8
    zero = jnp.zeros((16, 128), BF16)

    def double(x):
        return jnp.concatenate([x, x], 0).astype(BF16)

    def column(col, _):
        tx = col >> 2
        ty = col & 3
        depth[...] = jnp.zeros_like(depth)
        for pair in range(8):
            f = fields.at[pair]
            g = places.at[pair]
            high = data[tx, ty, pair].astype(F32)
            cell = cells[tx, ty, 2 * pair : 2 * pair + 2, :]
            f[0:8, :] = high
            f[8:16, :] = 1.0 - high
            g[0:2, :] = (cell >> 6).astype(F32)
            g[2:4, :] = ((cell >> 3) & 7).astype(F32)
            g[4:6, :] = ((cell & 7) + odd).astype(F32)
            left, right = [], []
            for half in range(2):
                def up(field, half=half):
                    return row8(f, 4 * half + field)

                def down(field, half=half):
                    return row8(f, 8 + 4 * half + field)

                def wide(x):
                    return jnp.concatenate([x, x], 0)

                mass = jnp.where(lane < counts[tx, ty, 2 * pair + half], up(0), 0.0)
                c0, c1 = double(down(3) * mass), double(up(3) * mass)
                x = wide(row8(g, half))
                f[16 + 16 * half : 32 + 16 * half, :] = jnp.where(
                    rows == x, wide(down(1)), jnp.where(rows - 1.0 == x, wide(up(1)), 0.0)
                )
                y, z = double(row8(g, 2 + half)), double(row8(g, 4 + half))
                along_y = jnp.where(
                    here == y, double(down(2)), jnp.where(before == y, double(up(2)), zero)
                )
                left.append(
                    jnp.concatenate(
                        [jnp.where(here == z, c0, jnp.where(before == z, c1, zero)),
                         jnp.where(fifteen == z, c1, zero)], 0
                    )
                )
                right.append(
                    jnp.concatenate(
                        [row16(f, 16 + 16 * half + k) * along_y for k in range(9)], 0
                    )
                )
            depth[16 * pair : 16 * pair + 32, 0:144] += dot_nt(
                jnp.concatenate(left, 1), jnp.concatenate(right, 1)
            )
        depth[0:16, :] += depth[128:144, :]
        first = jnp.transpose(depth[0:128, 0:128])
        final = jnp.transpose(depth[0:128, 128:256])
        at = pl.ds(pl.multiple_of(8 * ty, 8), 16)
        for k in range(8):
            grid[8 * tx + k, at, :] += first[16 * k : 16 * k + 16]
        grid[8 * tx + 8, at, :] += final[0:16]
        return 0

    lax.fori_loop(*columns, column, 0)


def first_kernel(
    counts, vcounts, tcounts, data_hbm, cells_hbm, vdata_hbm, vcells_hbm, tdata_hbm, tcells_hbm,
    toward, away, packs, core, face_y,
    data, cells, vdata, vcells, tdata, tcells, grid, tile_fields, tile_places, depth, total, fields, places, lines, number, sems,
):
    sources = [(tdata_hbm, tdata), (tcells_hbm, tcells), (vdata_hbm, vdata), (vcells_hbm, vcells)]
    for at, offset in enumerate(OUTER):
        here = pl.ds(16 * at, 16)
        sources.append((data_hbm.at[offset], data.at[here]))
        sources.append((cells_hbm.at[0, offset], cells.at[here]))
    copies = [
        pltpu.make_async_copy(source, target, sems.at[index])
        for index, (source, target) in enumerate(sources)
    ]
    for copy in copies:
        copy.start()
    grid[...] = jnp.zeros_like(grid)
    for copy in copies[:2]:
        copy.wait()
    deposit_tiles((3, 8), tcounts, tdata, tcells, grid, tile_fields, tile_places, depth)
    core[...] = grid[0:16, 0:32, :]
    face_y[...] = grid[0:16, 32, :]
    for copy in copies[2:4]:
        copy.wait()
    for offset in range(9):
        out = (toward, packs, away)[offset // 3]
        slot = offset % 3 if out is packs else 17 * (offset % 3) + 16
        out[slot] = pack_virtual(offset, vcounts, vdata, vcells, lines)
    high, low = high_low(grid[16, 0:32, :])
    away[51] = high
    away[52] = low
    high, low = high_low(
        jnp.concatenate([grid[16, 32:40, :], jnp.zeros((8, 128), F32)], 0)
    )
    away[53] = jnp.concatenate([high, low], 0)
    deposit_ghosts(
        OUTER,
        32,
        counts,
        lambda group, chunk: data[group, chunk],
        lambda group, at: cells[pl.ds(group, 1), pl.ds(at, LANES)],
        (toward, away),
        total,
        fields,
        places,
        number,
        copies[4:],
    )


def first_part(counts, vcounts, tcounts, data, cells, vdata, vcells, tdata, tcells):
    slots = cells.shape[3]
    patches = 16 * len(OUTER)
    full = pl.BlockSpec(memory_space=pltpu.VMEM)
    smem = pl.BlockSpec(memory_space=pltpu.SMEM)
    hbm = pl.BlockSpec(memory_space=pltpu.HBM)
    return pl.pallas_call(
        first_kernel,
        in_specs=[smem] * 3 + [hbm] * 6,
        out_specs=[full] * 5,
        scratch_shapes=[
            pltpu.VMEM((patches, slots // LANES, 8, 128), BF16),
            pltpu.VMEM((patches, slots), I32),
            pltpu.VMEM(vdata.shape, BF16),
            pltpu.VMEM(vcells.shape, I32),
            pltpu.VMEM(tdata.shape, BF16),
            pltpu.VMEM(tcells.shape, I32),
            pltpu.VMEM((17, 40, 128), F32),
            pltpu.VMEM((8, 48, 128), F32),
            pltpu.VMEM((8, 8, 128), F32),
            pltpu.VMEM((144, 256), F32),
            pltpu.VMEM((patches, 64, 128), F32),
            pltpu.VMEM((32, 32, 128), F32),
            pltpu.VMEM((32, 8, LANES), F32),
            pltpu.VMEM((32, 128), F32),
            pltpu.SMEM((patches + 36,), I32),
            pltpu.SemaphoreType.DMA((16,)),
        ],
        out_shape=[
            jax.ShapeDtypeStruct((51, 32, 128), BF16),
            jax.ShapeDtypeStruct((54, 32, 128), BF16),
            jax.ShapeDtypeStruct((3, 32, 128), BF16),
            jax.ShapeDtypeStruct((16, 32, 128), F32),
            jax.ShapeDtypeStruct((16, 128), F32),
        ],
        compiler_params=pltpu.CompilerParams(vmem_limit_bytes=FIRST_LIMIT),
        cost_estimate=pl.CostEstimate(
            flops=4 * patches * slots * 64 * 128, bytes_accessed=4000000, transcendentals=0
        ),
        name="first",
    )(counts, vcounts, tcounts, data, cells, vdata, vcells, tdata, tcells)


def own_kernel(
    offsets, counts, data, cells, wait, out, total, fields, places, number
):
    def split(group):
        return offsets[0] + 2 * (group >> 4), group & 15

    def get_data(group, chunk):
        offset, patch = split(group)
        return data[offset, patch, chunk]

    def get_cells(group, at):
        offset, patch = split(group)
        return cells[0, offset, pl.ds(patch, 1), pl.ds(at, LANES)]

    deposit_ghosts(
        offsets, 24, counts, get_data, get_cells, (out,), total, fields, places, number, ()
    )


def own_part(offsets, counts, data, cells, wait):
    slots = cells.shape[3]
    patches = 16 * len(offsets)
    full = pl.BlockSpec(memory_space=pltpu.VMEM)
    smem = pl.BlockSpec(memory_space=pltpu.SMEM)
    anywhere = pl.BlockSpec(memory_space=pl.ANY)
    return pl.pallas_call(
        functools.partial(own_kernel, offsets),
        in_specs=[smem, full, full, anywhere],
        out_specs=full,
        scratch_shapes=[
            pltpu.VMEM((patches, 64, 128), F32),
            pltpu.VMEM((24, 32, 128), F32),
            pltpu.VMEM((24, 8, LANES), F32),
            pltpu.SMEM((patches + 28,), I32),
        ],
        out_shape=jax.ShapeDtypeStruct((patches, 32, 128), BF16),
        compiler_params=pltpu.CompilerParams(vmem_limit_bytes=VMEM_LIMIT),
        cost_estimate=pl.CostEstimate(
            flops=4 * patches * slots * 64 * 128, bytes_accessed=4000000, transcendentals=0
        ),
        name="own",
    )(counts, data, cells, wait)


def virtual_deposit(packs, out, lines, fields):
    lanes = 512
    rows = sublane(16, lanes)
    zero = jnp.zeros((16, lanes), BF16)

    def place(at):
        return (rows + float(at)).astype(BF16)

    for which, (source, slot) in enumerate(packs):
        f = fields.at[which & 1]
        g = lines.at[which & 1]
        g[...] = source[slot].astype(F32)

        def value(field):
            return jnp.concatenate(
                [g[4 * field + quarter : 4 * field + quarter + 1, :] for quarter in range(4)], 1
            )

        cell = (value(4) * 256.0 + value(5)).astype(I32)
        mass, fx, fy, fz = value(0), value(1), value(2), value(3)
        f[0:1, :] = fx
        f[1:2, :] = 1.0 - fx
        f[2:3, :] = fy
        f[3:4, :] = 1.0 - fy
        f[4:5, :] = fz * mass
        f[5:6, :] = (1.0 - fz) * mass
        f[10:11, :] = (cell >> 12).astype(F32)
        f[11:12, :] = ((cell >> 7) & 31).astype(F32)
        f[12:13, :] = (cell & 127).astype(F32)
        f[13:14, :] = ((cell + 1) & 127).astype(F32)
        x = jnp.concatenate([row8(f, 10)] * 2, 0)
        low_x = jnp.concatenate([row8(f, 1)] * 2, 0)
        high_x = jnp.concatenate([row8(f, 0)] * 2, 0)
        f[16:32, :] = jnp.where(
            rows == x, low_x, jnp.where(rows - 1.0 == x, high_x, 0.0)
        )
        y, z, z_next = row16(f, 11), row16(f, 12), row16(f, 13)
        c0, c1 = row16(f, 5), row16(f, 4)
        y0, y1 = row16(f, 3), row16(f, 2)
        along_y = [
            jnp.where(place(16 * h) == y, y0, jnp.where(place(16 * h - 1) == y, y1, zero))
            for h in range(2)
        ]
        along_z = jnp.concatenate(
            [
                jnp.where(
                    place(16 * k) == z, c0, jnp.where(place(16 * k) == z_next, c1, zero)
                )
                for k in range(8)
            ],
            0,
        )
        left = []
        for k in range(16):
            w = row16(f, 16 + k)
            left += [w * along_y[0], w * along_y[1]]
        out[...] += dot_nt(jnp.concatenate(left, 0), along_z)


def base_kernel(
    tcounts, tdata, tcells, packs, right, left, core, out, lines, fields, grid, tile_fields,
    tile_places, depth
):
    grid[...] = jnp.zeros_like(grid)
    grid[0:16, 0:32, :] = core[...]
    deposit_tiles((0, 3), tcounts, tdata, tcells, grid, tile_fields, tile_places, depth)
    out[...] = grid[0:16, 0:32, :].reshape(512, 128)
    out[0:32, :] += left[51].astype(F32) + left[52].astype(F32)
    virtual_deposit([(packs, 1), (right, 33), (left, 33)], out, lines, fields)


def base_part(*args):
    full = pl.BlockSpec(memory_space=pltpu.VMEM)
    smem = pl.BlockSpec(memory_space=pltpu.SMEM)
    return pl.pallas_call(
        base_kernel,
        in_specs=[smem] + [full] * 6,
        out_specs=full,
        out_shape=jax.ShapeDtypeStruct((512, 128), F32),
        scratch_shapes=[
            pltpu.VMEM((2, 32, 128), F32),
            pltpu.VMEM((2, 32, 512), F32),
            pltpu.VMEM((17, 40, 128), F32),
            pltpu.VMEM((8, 48, 128), F32),
            pltpu.VMEM((8, 8, 128), F32),
            pltpu.VMEM((144, 256), F32),
        ],
        compiler_params=pltpu.CompilerParams(vmem_limit_bytes=VMEM_LIMIT),
        cost_estimate=pl.CostEstimate(
            flops=6 * 3 * 512 * 512 * 128, bytes_accessed=1000000, transcendentals=0
        ),
        name="base",
    )(*args)


def join_kernel(own, packs, right, left, face_y, up, down):
    for at, (out, slot) in enumerate(((up, 0), (down, 34))):
        for patch in range(16):
            out[patch] = (
                own[16 * at + patch].astype(F32)
                + right[slot + patch].astype(F32)
                + left[slot + patch].astype(F32)
            ).astype(BF16)
        out[16] = packs[2 * at]
        out[17] = right[slot + 16]
        out[18] = left[slot + 16]
    corner = left[53].astype(F32)
    row = lax.broadcasted_iota(I32, (16, 128), 0)
    face = face_y[...] + jnp.where(row == 0, corner[0:16] + corner[16:32], 0.0)
    high, low = high_low(face)
    down[19] = jnp.concatenate([high, low], 0)


def join_part(*args):
    full = pl.BlockSpec(memory_space=pltpu.VMEM)
    return pl.pallas_call(
        join_kernel,
        in_specs=[full] * 5,
        out_specs=[full] * 2,
        out_shape=[jax.ShapeDtypeStruct((size, 32, 128), BF16) for size in (19, 20)],
        compiler_params=pltpu.CompilerParams(vmem_limit_bytes=VMEM_LIMIT),
        name="join",
    )(*args)


def last_kernel(part, own, right, left, up, down, base, out, patches, fields, lines):
    for patch in range(16):
        mass = (
            (own[patch].astype(F32) + left[17 + patch].astype(F32))
            + (right[17 + patch].astype(F32) + up[patch].astype(F32))
        ) + down[patch].astype(F32)
        patches[32 * patch : 32 * patch + 32, :] = mass
    for group in range(2):
        for half in range(2):
            for x in range(16):
                block = patches[pl.ds(256 * group + 16 * half + x, 8, stride=32), :]
                at = 128 * (2 * x + half)
                out[8 * group : 8 * group + 8, at : at + 128] = block
    base[...] = part[...]
    both = down[19].astype(F32)
    face = both[0:16] + both[16:32]
    for x in range(16):
        base[32 * x : 32 * x + 1, :] += face[x : x + 1, :]
    virtual_deposit(
        [(source, slot) for source in (up, down) for slot in (16, 17, 18)], base, lines, fields
    )


def last_part(*args):
    full = pl.BlockSpec(memory_space=pltpu.VMEM)
    return pl.pallas_call(
        last_kernel,
        in_specs=[full] * 6,
        out_specs=[full] * 2,
        out_shape=[
            jax.ShapeDtypeStruct((512, 128), F32),
            jax.ShapeDtypeStruct((16, 4096), F32),
        ],
        scratch_shapes=[
            pltpu.VMEM((512, 128), F32),
            pltpu.VMEM((2, 32, 512), F32),
            pltpu.VMEM((2, 32, 128), F32),
        ],
        compiler_params=pltpu.CompilerParams(vmem_limit_bytes=VMEM_LIMIT),
        name="last",
    )(*args)


def on_device(
    part_data,
    tile_cells,
    tile_counts,
    ghost_data,
    halo_refined_cells,
    ghost_counts,
    virt_data,
    virt_cells,
    phantom_slot_counts,
):
    sources, own_patches, fields, slots = ghost_data.shape[1:]
    tiled = ghost_data.reshape(sources, own_patches, fields, slots // LANES, 2, 128)
    tiled = tiled.transpose(0, 1, 3, 4, 2, 5)
    tiled = tiled.reshape(sources, own_patches, slots // LANES, 8, 128)
    counts = jnp.swapaxes(ghost_counts, 0, 1)
    tiles = part_data.shape
    pairs = part_data.reshape(tiles[0], tiles[1], tiles[2] // 2, 8, tiles[4])
    toward, away, packs, core, face_y = first_part(
        counts,
        phantom_slot_counts,
        tile_counts,
        tiled,
        halo_refined_cells,
        virt_data,
        jnp.swapaxes(virt_cells, 0, 1),
        pairs,
        tile_cells,
    )
    right = shift(toward, "gx", -1)
    left = shift(away, "gx", 1)
    sides = own_part((3, 5), counts, tiled, halo_refined_cells, face_y)
    up, down = join_part(sides, packs, right, left, face_y)
    from_up = shift(up, "gy", -1)
    from_down = shift(down, "gy", 1)
    own = own_part((4,), counts, tiled, halo_refined_cells, down)
    part = base_part(tile_counts, pairs, tile_cells, packs, right, left, core)
    base, fine_mass = last_part(part, own, right, left, from_up, from_down)
    return base.reshape(16, 32, 128), fine_mass


def solution(mesh):
    return jax.shard_map(
        on_device,
        mesh=mesh,
        in_specs=(
            P("gx", "gy", None, None, None),
            P("gx", "gy", None, None),
            P("gx", "gy", None),
            P(("gx", "gy"), None, None, None, None),
            P(("gx", "gy"), None, None, None),
            P(("gx", "gy"), None, None),
            P(("gx", "gy"), None, None, None),
            P(("gx", "gy"), None, None),
            P(("gx", "gy"), None),
        ),
        out_specs=(P("gx", "gy", None), P(("gx", "gy"), None)),
        check_vma=False,
    )
```

```python
import functools

import jax
import jax.numpy as jnp
from jax import lax
from jax.experimental import pallas as pl
from jax.experimental.pallas import tpu as pltpu
from jax.sharding import PartitionSpec as P

BF16 = jnp.bfloat16
F32 = jnp.float32
I32 = jnp.int32
NT = (((1,), (1,)), ((), ()))
LANES = 256
FIRST_UNROLLS = (48, 16)
OWN_UNROLLS = (48, 16)
EXTRA = 64
OUTER = (0, 1, 2, 6, 7, 8)
VMEM_LIMIT = 16 * 2**20
FIRST_LIMIT = 56 * 2**20


def shift(x, axis, by):
    devices = lax.axis_size(axis)
    return lax.ppermute(x, axis, [(i, (i + by) % devices) for i in range(devices)])


def sublane(rows, lanes):
    return lax.broadcasted_iota(I32, (rows, lanes), 0).astype(F32)


def dot_nt(a, b):
    return lax.dot_general(a, b, NT, preferred_element_type=F32)


def row8(ref, row):
    return ref[pl.ds(row, 8, stride=0), :]


def row16(ref, row):
    return jnp.concatenate([row8(ref, row)] * 2, 0).astype(BF16)


def high_low(x):
    high = x.astype(BF16)
    return high, (x - high.astype(F32)).astype(BF16)


def pack_virtual(offset, counts, data, cells, lines):
    lane = lax.broadcasted_iota(I32, (1, 512), 1)
    high = data[0, offset].astype(F32)
    cell = cells[offset]
    values = [
        jnp.where(lane < counts[0, offset], high[0:1], 0.0),
        high[1:2],
        high[2:3],
        high[3:4],
        (cell >> 8).astype(F32),
        (cell & 255).astype(F32),
    ]
    for field, value in enumerate(values):
        for quarter in range(4):
            at = 4 * field + quarter
            lines[at : at + 1, :] = value[:, 128 * quarter : 128 * quarter + 128]
    lines[24:32, :] = jnp.zeros((8, 128), F32)
    return lines[...].astype(BF16)


def deposit_ghosts(offsets, unrolls, counts, get_data, get_cells, outs, total, fields, places, number, ready):
    split = len(outs)
    patches = 16 * len(offsets)
    each = len(offsets) // split
    total[...] = jnp.zeros_like(total)
    work = jnp.int32(0)
    for at, offset in enumerate(offsets):
        for patch in range(16):
            live = counts[offset, 0, patch]
            number[16 * at + patch] = live
            work = work + jnp.maximum((live + (LANES - 1)) >> 8, 1)
    for extra in range(EXTRA):
        number[patches + extra] = 0
    lane = lax.broadcasted_iota(I32, (8, 128), 1)
    here = sublane(16, 128).astype(BF16)
    before = (sublane(16, 128) - 1.0).astype(BF16)
    rows = sublane(8, 128)
    zero = jnp.zeros((16, 128), BF16)
    for copy in ready:
        copy.wait()

    def deposit(unit, group, start, live, next_one, next_two):
        patch = jnp.minimum(group, patches - 1)
        at = pl.multiple_of(start, LANES)
        high = get_data(patch, start >> 8).astype(F32)
        cell = get_cells(patch, at)
        f = fields.at[unit]
        g = places.at[unit]
        f[0:8, :] = high
        f[8:16, :] = 1.0 - high
        g[0:1, :] = (cell >> 8).astype(F32)
        g[1:2, :] = (cell & 15).astype(F32)
        g[2:3, :] = ((cell >> 4) & 3).astype(F32)
        g[3:4, :] = ((cell >> 6) & 3).astype(F32)
        left, right = [], []
        for half in range(2):
            wide = slice(128 * half, 128 * half + 128)

            def up(field, half=half):
                return row8(f, 4 * half + field)

            def down(field, half=half):
                return row8(f, 8 + 4 * half + field)

            def double(x):
                return jnp.concatenate([x, x], 0).astype(BF16)

            def where_at(field, wide=wide):
                return g[pl.ds(field, 8, stride=0), :][:, wide]

            mass = jnp.where(lane < live - 128 * half, up(0), 0.0)
            c0, c1 = double(down(3) * mass), double(up(3) * mass)
            x0, x1 = double(down(1)), double(up(1))
            inner = where_at(2)
            f[16 + 8 * half : 24 + 8 * half, :] = jnp.where(
                rows == inner, down(2), jnp.where(rows - 1.0 == inner, up(2), 0.0)
            )
            x, z, outer = double(where_at(0)), double(where_at(1)), double(where_at(3))
            along_x = jnp.where(here == x, x0, jnp.where(before == x, x1, zero))
            along_z = jnp.where(here == z, c0, jnp.where(before == z, c1, zero))
            left.append(
                jnp.concatenate(
                    [jnp.where(outer == BF16(k), along_x, zero) for k in range(4)], 0
                )
            )
            right.append(
                jnp.concatenate(
                    [row16(f, 16 + 8 * half + k) * along_z for k in range(5)], 0
                )
            )
        total[patch, :, 0:80] += dot_nt(
            jnp.concatenate(left, 1), jnp.concatenate(right, 1)
        )
        last = live <= LANES
        group = jnp.where(last, group + 1, group)
        return (
            group,
            jnp.where(last, 0, start + LANES),
            jnp.where(last, next_one, live - LANES),
            jnp.where(last, next_two, next_one),
            number[group + 2],
        )

    none = jnp.int32(0)
    state = (none, none, number[0], number[1], number[2])
    for unroll in unrolls:
        if unroll == unrolls[-1]:
            steps = lax.div(work + (unroll - 1), unroll)
        else:
            steps = lax.div(work, unroll)
            work = work - steps * unroll

        def body(_, state, unroll=unroll):
            for unit in range(unroll):
                state = deposit(unit, *state)
            return state

        state = lax.fori_loop(0, steps, body, state)
    lane = lax.broadcasted_iota(I32, (16, 128), 1)

    for index in range(split):
        out = outs[index]

        def fold(k, _, index=index, out=out):
            group = 16 * each * index + k
            for half in range(2):
                at = 32 * half
                even = total[group, at : at + 16]
                odd = total[group, at + 16 : at + 32]
                prior = total[group, at - 16 : at] if half else jnp.zeros((16, 128), F32)
                swapped = pltpu.roll(jnp.where(lane < 64, odd, prior), 64, 1)
                out[k + (k >> 4) if split > 1 else k, 16 * half : 16 * half + 16] = (even + swapped).astype(BF16)
            return 0

        lax.fori_loop(0, 16 * each, fold, 0, unroll=8)


def deposit_tiles(columns, counts, data, cells, grid, fields, places, depth):
    lane = lax.broadcasted_iota(I32, (8, 128), 1)
    here = sublane(16, 128).astype(BF16)
    before = (sublane(16, 128) - 1.0).astype(BF16)
    fifteen = (sublane(16, 128) + 15.0).astype(BF16)
    rows = sublane(16, 128)
    odd = lax.broadcasted_iota(I32, (2, 128), 0) * 8
    zero = jnp.zeros((16, 128), BF16)

    def double(x):
        return jnp.concatenate([x, x], 0).astype(BF16)

    def column(col, _):
        tx = col >> 2
        ty = col & 3
        depth[...] = jnp.zeros_like(depth)
        for pair in range(8):
            f = fields.at[pair]
            g = places.at[pair]
            high = data[tx, ty, pair].astype(F32)
            cell = cells[tx, ty, 2 * pair : 2 * pair + 2, :]
            f[0:8, :] = high
            f[8:16, :] = 1.0 - high
            g[0:2, :] = (cell >> 6).astype(F32)
            g[2:4, :] = ((cell >> 3) & 7).astype(F32)
            g[4:6, :] = ((cell & 7) + odd).astype(F32)
            left, right = [], []
            for half in range(2):
                def up(field, half=half):
                    return row8(f, 4 * half + field)

                def down(field, half=half):
                    return row8(f, 8 + 4 * half + field)

                def wide(x):
                    return jnp.concatenate([x, x], 0)

                mass = jnp.where(lane < counts[tx, ty, 2 * pair + half], up(0), 0.0)
                c0, c1 = double(down(3) * mass), double(up(3) * mass)
                x = wide(row8(g, half))
                f[16 + 16 * half : 32 + 16 * half, :] = jnp.where(
                    rows == x, wide(down(1)), jnp.where(rows - 1.0 == x, wide(up(1)), 0.0)
                )
                y, z = double(row8(g, 2 + half)), double(row8(g, 4 + half))
                along_y = jnp.where(
                    here == y, double(down(2)), jnp.where(before == y, double(up(2)), zero)
                )
                left.append(
                    jnp.concatenate(
                        [jnp.where(here == z, c0, jnp.where(before == z, c1, zero)),
                         jnp.where(fifteen == z, c1, zero)], 0
                    )
                )
                right.append(
                    jnp.concatenate(
                        [row16(f, 16 + 16 * half + k) * along_y for k in range(9)], 0
                    )
                )
            depth[16 * pair : 16 * pair + 32, 0:144] += dot_nt(
                jnp.concatenate(left, 1), jnp.concatenate(right, 1)
            )
        depth[0:16, :] += depth[128:144, :]
        first = jnp.transpose(depth[0:128, 0:128])
        final = jnp.transpose(depth[0:128, 128:256])
        at = pl.ds(pl.multiple_of(8 * ty, 8), 16)
        for k in range(8):
            grid[8 * tx + k, at, :] += first[16 * k : 16 * k + 16]
        grid[8 * tx + 8, at, :] += final[0:16]
        return 0

    lax.fori_loop(*columns, column, 0)


def first_kernel(
    counts, vcounts, tcounts, data_hbm, cells_hbm, vdata_hbm, vcells_hbm, tdata_hbm, tcells_hbm,
    toward, away, packs, core, face_y,
    data, cells, vdata, vcells, tdata, tcells, grid, tile_fields, tile_places, depth, total, fields, places, lines, number, sems,
):
    sources = [(tdata_hbm, tdata), (tcells_hbm, tcells), (vdata_hbm, vdata), (vcells_hbm, vcells)]
    for at, offset in enumerate(OUTER):
        here = pl.ds(16 * at, 16)
        sources.append((data_hbm.at[offset], data.at[here]))
        sources.append((cells_hbm.at[0, offset], cells.at[here]))
    copies = [
        pltpu.make_async_copy(source, target, sems.at[index])
        for index, (source, target) in enumerate(sources)
    ]
    for copy in copies:
        copy.start()
    grid[...] = jnp.zeros_like(grid)
    for copy in copies[:2]:
        copy.wait()
    deposit_tiles((3, 8), tcounts, tdata, tcells, grid, tile_fields, tile_places, depth)
    core[...] = grid[0:16, 0:32, :]
    face_y[...] = grid[0:16, 32, :]
    for copy in copies[2:4]:
        copy.wait()
    for offset in range(9):
        out = (toward, packs, away)[offset // 3]
        slot = offset % 3 if out is packs else 17 * (offset % 3) + 16
        out[slot] = pack_virtual(offset, vcounts, vdata, vcells, lines)
    high, low = high_low(grid[16, 0:32, :])
    away[51] = high
    away[52] = low
    high, low = high_low(
        jnp.concatenate([grid[16, 32:40, :], jnp.zeros((8, 128), F32)], 0)
    )
    away[53] = jnp.concatenate([high, low], 0)
    deposit_ghosts(
        OUTER,
        FIRST_UNROLLS,
        counts,
        lambda group, chunk: data[group, chunk],
        lambda group, at: cells[pl.ds(group, 1), pl.ds(at, LANES)],
        (toward, away),
        total,
        fields,
        places,
        number,
        copies[4:],
    )


def first_part(counts, vcounts, tcounts, data, cells, vdata, vcells, tdata, tcells):
    slots = cells.shape[3]
    patches = 16 * len(OUTER)
    full = pl.BlockSpec(memory_space=pltpu.VMEM)
    smem = pl.BlockSpec(memory_space=pltpu.SMEM)
    hbm = pl.BlockSpec(memory_space=pltpu.HBM)
    return pl.pallas_call(
        first_kernel,
        in_specs=[smem] * 3 + [hbm] * 6,
        out_specs=[full] * 5,
        scratch_shapes=[
            pltpu.VMEM((patches, slots // LANES, 8, 128), BF16),
            pltpu.VMEM((patches, slots), I32),
            pltpu.VMEM(vdata.shape, BF16),
            pltpu.VMEM(vcells.shape, I32),
            pltpu.VMEM(tdata.shape, BF16),
            pltpu.VMEM(tcells.shape, I32),
            pltpu.VMEM((17, 40, 128), F32),
            pltpu.VMEM((8, 48, 128), F32),
            pltpu.VMEM((8, 8, 128), F32),
            pltpu.VMEM((144, 256), F32),
            pltpu.VMEM((patches, 64, 128), F32),
            pltpu.VMEM((max(FIRST_UNROLLS), 32, 128), F32),
            pltpu.VMEM((max(FIRST_UNROLLS), 8, LANES), F32),
            pltpu.VMEM((32, 128), F32),
            pltpu.SMEM((patches + EXTRA,), I32),
            pltpu.SemaphoreType.DMA((16,)),
        ],
        out_shape=[
            jax.ShapeDtypeStruct((51, 32, 128), BF16),
            jax.ShapeDtypeStruct((54, 32, 128), BF16),
            jax.ShapeDtypeStruct((3, 32, 128), BF16),
            jax.ShapeDtypeStruct((16, 32, 128), F32),
            jax.ShapeDtypeStruct((16, 128), F32),
        ],
        compiler_params=pltpu.CompilerParams(vmem_limit_bytes=FIRST_LIMIT),
        cost_estimate=pl.CostEstimate(
            flops=4 * patches * slots * 64 * 128, bytes_accessed=4000000, transcendentals=0
        ),
        name="first",
    )(counts, vcounts, tcounts, data, cells, vdata, vcells, tdata, tcells)


def own_kernel(
    offsets, counts, data, cells, wait, out, total, fields, places, number
):
    def split(group):
        return offsets[0] + 2 * (group >> 4), group & 15

    def get_data(group, chunk):
        offset, patch = split(group)
        return data[offset, patch, chunk]

    def get_cells(group, at):
        offset, patch = split(group)
        return cells[0, offset, pl.ds(patch, 1), pl.ds(at, LANES)]

    deposit_ghosts(
        offsets, OWN_UNROLLS, counts, get_data, get_cells, (out,), total, fields, places, number, ()
    )


def own_part(offsets, counts, data, cells, wait):
    slots = cells.shape[3]
    patches = 16 * len(offsets)
    full = pl.BlockSpec(memory_space=pltpu.VMEM)
    smem = pl.BlockSpec(memory_space=pltpu.SMEM)
    anywhere = pl.BlockSpec(memory_space=pl.ANY)
    return pl.pallas_call(
        functools.partial(own_kernel, offsets),
        in_specs=[smem, full, full, anywhere],
        out_specs=full,
        scratch_shapes=[
            pltpu.VMEM((patches, 64, 128), F32),
            pltpu.VMEM((max(OWN_UNROLLS), 32, 128), F32),
            pltpu.VMEM((max(OWN_UNROLLS), 8, LANES), F32),
            pltpu.SMEM((patches + EXTRA,), I32),
        ],
        out_shape=jax.ShapeDtypeStruct((patches, 32, 128), BF16),
        compiler_params=pltpu.CompilerParams(vmem_limit_bytes=VMEM_LIMIT),
        cost_estimate=pl.CostEstimate(
            flops=4 * patches * slots * 64 * 128, bytes_accessed=4000000, transcendentals=0
        ),
        name="own",
    )(counts, data, cells, wait)


def virtual_deposit(packs, out, lines, fields):
    lanes = 512
    rows = sublane(16, lanes)
    zero = jnp.zeros((16, lanes), BF16)

    def place(at):
        return (rows + float(at)).astype(BF16)

    for which, (source, slot) in enumerate(packs):
        f = fields.at[which & 1]
        g = lines.at[which & 1]
        g[...] = source[slot].astype(F32)

        def value(field):
            return jnp.concatenate(
                [g[4 * field + quarter : 4 * field + quarter + 1, :] for quarter in range(4)], 1
            )

        cell = (value(4) * 256.0 + value(5)).astype(I32)
        mass, fx, fy, fz = value(0), value(1), value(2), value(3)
        f[0:1, :] = fx
        f[1:2, :] = 1.0 - fx
        f[2:3, :] = fy
        f[3:4, :] = 1.0 - fy
        f[4:5, :] = fz * mass
        f[5:6, :] = (1.0 - fz) * mass
        f[10:11, :] = (cell >> 12).astype(F32)
        f[11:12, :] = ((cell >> 7) & 31).astype(F32)
        f[12:13, :] = (cell & 127).astype(F32)
        f[13:14, :] = ((cell + 1) & 127).astype(F32)
        x = jnp.concatenate([row8(f, 10)] * 2, 0)
        low_x = jnp.concatenate([row8(f, 1)] * 2, 0)
        high_x = jnp.concatenate([row8(f, 0)] * 2, 0)
        f[16:32, :] = jnp.where(
            rows == x, low_x, jnp.where(rows - 1.0 == x, high_x, 0.0)
        )
        y, z, z_next = row16(f, 11), row16(f, 12), row16(f, 13)
        c0, c1 = row16(f, 5), row16(f, 4)
        y0, y1 = row16(f, 3), row16(f, 2)
        along_y = [
            jnp.where(place(16 * h) == y, y0, jnp.where(place(16 * h - 1) == y, y1, zero))
            for h in range(2)
        ]
        along_z = jnp.concatenate(
            [
                jnp.where(
                    place(16 * k) == z, c0, jnp.where(place(16 * k) == z_next, c1, zero)
                )
                for k in range(8)
            ],
            0,
        )
        left = []
        for k in range(16):
            w = row16(f, 16 + k)
            left += [w * along_y[0], w * along_y[1]]
        out[...] += dot_nt(jnp.concatenate(left, 0), along_z)


def base_kernel(
    tcounts, tdata, tcells, packs, right, left, core, out, lines, fields, grid, tile_fields,
    tile_places, depth
):
    grid[...] = jnp.zeros_like(grid)
    grid[0:16, 0:32, :] = core[...]
    deposit_tiles((0, 3), tcounts, tdata, tcells, grid, tile_fields, tile_places, depth)
    out[...] = grid[0:16, 0:32, :].reshape(512, 128)
    out[0:32, :] += left[51].astype(F32) + left[52].astype(F32)
    virtual_deposit([(packs, 1), (right, 33), (left, 33)], out, lines, fields)


def base_part(*args):
    full = pl.BlockSpec(memory_space=pltpu.VMEM)
    smem = pl.BlockSpec(memory_space=pltpu.SMEM)
    return pl.pallas_call(
        base_kernel,
        in_specs=[smem] + [full] * 6,
        out_specs=full,
        out_shape=jax.ShapeDtypeStruct((512, 128), F32),
        scratch_shapes=[
            pltpu.VMEM((2, 32, 128), F32),
            pltpu.VMEM((2, 32, 512), F32),
            pltpu.VMEM((17, 40, 128), F32),
            pltpu.VMEM((8, 48, 128), F32),
            pltpu.VMEM((8, 8, 128), F32),
            pltpu.VMEM((144, 256), F32),
        ],
        compiler_params=pltpu.CompilerParams(vmem_limit_bytes=VMEM_LIMIT),
        cost_estimate=pl.CostEstimate(
            flops=6 * 3 * 512 * 512 * 128, bytes_accessed=1000000, transcendentals=0
        ),
        name="base",
    )(*args)


def join_kernel(own, packs, right, left, face_y, up, down):
    for at, (out, slot) in enumerate(((up, 0), (down, 34))):
        for patch in range(16):
            out[patch] = (
                own[16 * at + patch].astype(F32)
                + right[slot + patch].astype(F32)
                + left[slot + patch].astype(F32)
            ).astype(BF16)
        out[16] = packs[2 * at]
        out[17] = right[slot + 16]
        out[18] = left[slot + 16]
    corner = left[53].astype(F32)
    row = lax.broadcasted_iota(I32, (16, 128), 0)
    face = face_y[...] + jnp.where(row == 0, corner[0:16] + corner[16:32], 0.0)
    high, low = high_low(face)
    down[19] = jnp.concatenate([high, low], 0)


def join_part(*args):
    full = pl.BlockSpec(memory_space=pltpu.VMEM)
    return pl.pallas_call(
        join_kernel,
        in_specs=[full] * 5,
        out_specs=[full] * 2,
        out_shape=[jax.ShapeDtypeStruct((size, 32, 128), BF16) for size in (19, 20)],
        compiler_params=pltpu.CompilerParams(vmem_limit_bytes=VMEM_LIMIT),
        name="join",
    )(*args)


def last_kernel(
    part, own, right, left, up, down, base_hbm, out_hbm, patches, fields, lines, base, out, sems
):
    for patch in range(16):
        mass = (
            (own[patch].astype(F32) + left[17 + patch].astype(F32))
            + (right[17 + patch].astype(F32) + up[patch].astype(F32))
        ) + down[patch].astype(F32)
        patches[32 * patch : 32 * patch + 32, :] = mass
    for group in range(2):
        for half in range(2):
            for x in range(16):
                block = patches[pl.ds(256 * group + 16 * half + x, 8, stride=32), :]
                at = 128 * (2 * x + half)
                out[8 * group : 8 * group + 8, at : at + 128] = block
    fine_copy = pltpu.make_async_copy(out, out_hbm, sems.at[0])
    fine_copy.start()
    base[...] = part[...]
    both = down[19].astype(F32)
    face = both[0:16] + both[16:32]
    for x in range(16):
        base[32 * x : 32 * x + 1, :] += face[x : x + 1, :]
    virtual_deposit(
        [(source, slot) for source in (up, down) for slot in (16, 17, 18)], base, lines, fields
    )
    base_copy = pltpu.make_async_copy(base, base_hbm, sems.at[1])
    base_copy.start()
    fine_copy.wait()
    base_copy.wait()


def last_part(*args):
    full = pl.BlockSpec(memory_space=pltpu.VMEM)
    return pl.pallas_call(
        last_kernel,
        in_specs=[full] * 6,
        out_specs=[pl.BlockSpec(memory_space=pl.ANY)] * 2,
        out_shape=[
            jax.ShapeDtypeStruct((512, 128), F32),
            jax.ShapeDtypeStruct((16, 4096), F32),
        ],
        scratch_shapes=[
            pltpu.VMEM((512, 128), F32),
            pltpu.VMEM((2, 32, 512), F32),
            pltpu.VMEM((2, 32, 128), F32),
            pltpu.VMEM((512, 128), F32),
            pltpu.VMEM((16, 4096), F32),
            pltpu.SemaphoreType.DMA((2,)),
        ],
        compiler_params=pltpu.CompilerParams(vmem_limit_bytes=VMEM_LIMIT),
        name="last",
    )(*args)


def on_device(
    part_data,
    tile_cells,
    tile_counts,
    ghost_data,
    halo_refined_cells,
    ghost_counts,
    virt_data,
    virt_cells,
    phantom_slot_counts,
):
    sources, own_patches, fields, slots = ghost_data.shape[1:]
    tiled = ghost_data.reshape(sources, own_patches, fields, slots // LANES, 2, 128)
    tiled = tiled.transpose(0, 1, 3, 4, 2, 5)
    tiled = tiled.reshape(sources, own_patches, slots // LANES, 8, 128)
    counts = jnp.swapaxes(ghost_counts, 0, 1)
    tiles = part_data.shape
    pairs = part_data.reshape(tiles[0], tiles[1], tiles[2] // 2, 8, tiles[4])
    toward, away, packs, core, face_y = first_part(
        counts,
        phantom_slot_counts,
        tile_counts,
        tiled,
        halo_refined_cells,
        virt_data,
        jnp.swapaxes(virt_cells, 0, 1),
        pairs,
        tile_cells,
    )
    right = shift(toward, "gx", -1)
    left = shift(away, "gx", 1)
    sides = own_part((3, 5), counts, tiled, halo_refined_cells, face_y)
    up, down = join_part(sides, packs, right, left, face_y)
    from_up = shift(up, "gy", -1)
    from_down = shift(down, "gy", 1)
    own = own_part((4,), counts, tiled, halo_refined_cells, down)
    part = base_part(tile_counts, pairs, tile_cells, packs, right, left, core)
    base, fine_mass = last_part(part, own, right, left, from_up, from_down)
    return base.reshape(16, 32, 128), fine_mass


def solution(mesh):
    return jax.shard_map(
        on_device,
        mesh=mesh,
        in_specs=(
            P("gx", "gy", None, None, None),
            P("gx", "gy", None, None),
            P("gx", "gy", None),
            P(("gx", "gy"), None, None, None, None),
            P(("gx", "gy"), None, None, None),
            P(("gx", "gy"), None, None),
            P(("gx", "gy"), None, None, None),
            P(("gx", "gy"), None, None),
            P(("gx", "gy"), None),
        ),
        out_specs=(P("gx", "gy", None), P(("gx", "gy"), None)),
        check_vma=False,
    )
```

```python
import functools

import jax
import jax.numpy as jnp
from jax import lax
from jax.experimental import pallas as pl
from jax.experimental.pallas import tpu as pltpu
from jax.sharding import PartitionSpec as P

BF16 = jnp.bfloat16
F32 = jnp.float32
I32 = jnp.int32
NT = (((1,), (1,)), ((), ()))
LANES = 256
FIRST_UNROLLS = (48, 16)
OWN_UNROLLS = (48, 16)
EXTRA = 64
OUTER = (0, 1, 2, 6, 7, 8)
VMEM_LIMIT = 16 * 2**20
FIRST_LIMIT = 56 * 2**20


def shift(x, axis, by):
    devices = lax.axis_size(axis)
    return lax.ppermute(x, axis, [(i, (i + by) % devices) for i in range(devices)])


def sublane(rows, lanes):
    return lax.broadcasted_iota(I32, (rows, lanes), 0).astype(F32)


def dot_nt(a, b):
    return lax.dot_general(a, b, NT, preferred_element_type=F32)


def row8(ref, row):
    return ref[pl.ds(row, 8, stride=0), :]


def row16(ref, row):
    return jnp.concatenate([row8(ref, row)] * 2, 0).astype(BF16)


def high_low(x):
    high = x.astype(BF16)
    return high, (x - high.astype(F32)).astype(BF16)


def pack_virtual(offset, counts, data, cells, lines):
    lane = lax.broadcasted_iota(I32, (1, 512), 1)
    high = data[0, offset].astype(F32)
    cell = cells[offset]
    values = [
        jnp.where(lane < counts[0, offset], high[0:1], 0.0),
        high[1:2],
        high[2:3],
        high[3:4],
        (cell >> 8).astype(F32),
        (cell & 255).astype(F32),
    ]
    for field, value in enumerate(values):
        for quarter in range(4):
            at = 4 * field + quarter
            lines[at : at + 1, :] = value[:, 128 * quarter : 128 * quarter + 128]
    lines[24:32, :] = jnp.zeros((8, 128), F32)
    return lines[...].astype(BF16)


def deposit_ghosts(offsets, unrolls, counts, get_data, get_cells, outs, total, fields, places, number, ready):
    split = len(outs)
    patches = 16 * len(offsets)
    each = len(offsets) // split
    work = jnp.int32(0)
    for at, offset in enumerate(offsets):
        for patch in range(16):
            live = counts[offset, 0, patch]
            number[16 * at + patch] = live
            work = work + jnp.maximum((live + (LANES - 1)) >> 8, 1)
    for extra in range(EXTRA):
        number[patches + extra] = 0
    lane = lax.broadcasted_iota(I32, (8, 128), 1)
    here = sublane(16, 128).astype(BF16)
    before = (sublane(16, 128) - 1.0).astype(BF16)
    rows = sublane(8, 128)
    zero = jnp.zeros((16, 128), BF16)
    for copy in ready:
        copy.wait()

    def deposit(unit, group, start, live, next_one, next_two):
        patch = jnp.minimum(group, patches - 1)
        at = pl.multiple_of(start, LANES)
        high = get_data(patch, start >> 8).astype(F32)
        cell = get_cells(patch, at)
        f = fields.at[unit]
        g = places.at[unit]
        f[0:8, :] = high
        f[8:16, :] = 1.0 - high
        g[0:1, :] = (cell >> 8).astype(F32)
        g[1:2, :] = (cell & 15).astype(F32)
        g[2:3, :] = ((cell >> 4) & 3).astype(F32)
        g[3:4, :] = ((cell >> 6) & 3).astype(F32)
        left, right = [], []
        for half in range(2):
            wide = slice(128 * half, 128 * half + 128)

            def up(field, half=half):
                return row8(f, 4 * half + field)

            def down(field, half=half):
                return row8(f, 8 + 4 * half + field)

            def double(x):
                return jnp.concatenate([x, x], 0).astype(BF16)

            def where_at(field, wide=wide):
                return g[pl.ds(field, 8, stride=0), :][:, wide]

            mass = jnp.where(lane < live - 128 * half, up(0), 0.0)
            c0, c1 = double(down(3) * mass), double(up(3) * mass)
            x0, x1 = double(down(1)), double(up(1))
            inner = where_at(2)
            f[16 + 8 * half : 24 + 8 * half, :] = jnp.where(
                rows == inner, down(2), jnp.where(rows - 1.0 == inner, up(2), 0.0)
            )
            x, z, outer = double(where_at(0)), double(where_at(1)), double(where_at(3))
            along_x = jnp.where(here == x, x0, jnp.where(before == x, x1, zero))
            along_z = jnp.where(here == z, c0, jnp.where(before == z, c1, zero))
            left.append(
                jnp.concatenate(
                    [jnp.where(outer == BF16(k), along_x, zero) for k in range(4)], 0
                )
            )
            right.append(
                jnp.concatenate(
                    [row16(f, 16 + 8 * half + k) * along_z for k in range(5)], 0
                )
            )
        total[patch, :, 0:80] += dot_nt(
            jnp.concatenate(left, 1), jnp.concatenate(right, 1)
        )
        last = live <= LANES
        group = jnp.where(last, group + 1, group)
        return (
            group,
            jnp.where(last, 0, start + LANES),
            jnp.where(last, next_one, live - LANES),
            jnp.where(last, next_two, next_one),
            number[group + 2],
        )

    none = jnp.int32(0)
    state = (none, none, number[0], number[1], number[2])
    for unroll in unrolls:
        if unroll == unrolls[-1]:
            steps = lax.div(work + (unroll - 1), unroll)
        else:
            steps = lax.div(work, unroll)
            work = work - steps * unroll

        def body(_, state, unroll=unroll):
            for unit in range(unroll):
                state = deposit(unit, *state)
            return state

        state = lax.fori_loop(0, steps, body, state)
    lane = lax.broadcasted_iota(I32, (16, 128), 1)

    for index in range(split):
        out = outs[index]

        def fold(k, _, index=index, out=out):
            group = 16 * each * index + k
            for half in range(2):
                at = 32 * half
                even = total[group, at : at + 16]
                odd = total[group, at + 16 : at + 32]
                prior = total[group, at - 16 : at] if half else jnp.zeros((16, 128), F32)
                swapped = pltpu.roll(jnp.where(lane < 64, odd, prior), 64, 1)
                out[k + (k >> 4) if split > 1 else k, 16 * half : 16 * half + 16] = (even + swapped).astype(BF16)
            return 0

        lax.fori_loop(0, 16 * each, fold, 0, unroll=16)


def deposit_tiles(columns, counts, data, cells, grid, fields, places, depth, total=None):
    lane = lax.broadcasted_iota(I32, (8, 128), 1)
    here = sublane(16, 128).astype(BF16)
    before = (sublane(16, 128) - 1.0).astype(BF16)
    fifteen = (sublane(16, 128) + 15.0).astype(BF16)
    rows = sublane(16, 128)
    odd = lax.broadcasted_iota(I32, (2, 128), 0) * 8
    zero = jnp.zeros((16, 128), BF16)

    def double(x):
        return jnp.concatenate([x, x], 0).astype(BF16)

    def column(col, _):
        tx = col >> 2
        ty = col & 3
        depth[...] = jnp.zeros_like(depth)
        if total is not None:
            patches = total.shape[0]
            share = -(-patches // (columns[1] - columns[0]))
            begin = jnp.minimum((col - columns[0]) * share, patches - share)
            total[pl.ds(begin, share)] = jnp.zeros((share,) + total.shape[1:], F32)
        for pair in range(8):
            f = fields.at[pair]
            g = places.at[pair]
            high = data[tx, ty, pair].astype(F32)
            cell = cells[tx, ty, 2 * pair : 2 * pair + 2, :]
            f[0:8, :] = high
            f[8:16, :] = 1.0 - high
            g[0:2, :] = (cell >> 6).astype(F32)
            g[2:4, :] = ((cell >> 3) & 7).astype(F32)
            g[4:6, :] = ((cell & 7) + odd).astype(F32)
            left, right = [], []
            for half in range(2):
                def up(field, half=half):
                    return row8(f, 4 * half + field)

                def down(field, half=half):
                    return row8(f, 8 + 4 * half + field)

                def wide(x):
                    return jnp.concatenate([x, x], 0)

                mass = jnp.where(lane < counts[tx, ty, 2 * pair + half], up(0), 0.0)
                c0, c1 = double(down(3) * mass), double(up(3) * mass)
                x = wide(row8(g, half))
                f[16 + 16 * half : 32 + 16 * half, :] = jnp.where(
                    rows == x, wide(down(1)), jnp.where(rows - 1.0 == x, wide(up(1)), 0.0)
                )
                y, z = double(row8(g, 2 + half)), double(row8(g, 4 + half))
                along_y = jnp.where(
                    here == y, double(down(2)), jnp.where(before == y, double(up(2)), zero)
                )
                left.append(
                    jnp.concatenate(
                        [jnp.where(here == z, c0, jnp.where(before == z, c1, zero)),
                         jnp.where(fifteen == z, c1, zero)], 0
                    )
                )
                right.append(
                    jnp.concatenate(
                        [row16(f, 16 + 16 * half + k) * along_y for k in range(9)], 0
                    )
                )
            depth[16 * pair : 16 * pair + 32, 0:144] += dot_nt(
                jnp.concatenate(left, 1), jnp.concatenate(right, 1)
            )
        depth[0:16, :] += depth[128:144, :]
        first = jnp.transpose(depth[0:128, 0:128])
        final = jnp.transpose(depth[0:128, 128:256])
        at = pl.ds(pl.multiple_of(8 * ty, 8), 16)
        for k in range(8):
            grid[8 * tx + k, at, :] += first[16 * k : 16 * k + 16]
        grid[8 * tx + 8, at, :] += final[0:16]
        return 0

    lax.fori_loop(*columns, column, 0)


def first_kernel(
    counts, vcounts, tcounts, data_hbm, cells_hbm, vdata_hbm, vcells_hbm, tdata_hbm, tcells_hbm,
    toward, away, packs, core, face_y,
    data, cells, vdata, vcells, tdata, tcells, grid, tile_fields, tile_places, depth, total, fields, places, lines, number, sems,
):
    sources = [(tdata_hbm, tdata), (tcells_hbm, tcells), (vdata_hbm, vdata), (vcells_hbm, vcells)]
    for at, offset in enumerate(OUTER):
        here = pl.ds(16 * at, 16)
        sources.append((data_hbm.at[offset], data.at[here]))
        sources.append((cells_hbm.at[0, offset], cells.at[here]))
    copies = [
        pltpu.make_async_copy(source, target, sems.at[index])
        for index, (source, target) in enumerate(sources)
    ]
    for copy in copies:
        copy.start()
    grid[...] = jnp.zeros_like(grid)
    for copy in copies[:2]:
        copy.wait()
    deposit_tiles((3, 8), tcounts, tdata, tcells, grid, tile_fields, tile_places, depth, total)
    core[...] = grid[0:16, 0:32, :]
    face_y[...] = grid[0:16, 32, :]
    for copy in copies[2:4]:
        copy.wait()
    for offset in range(9):
        out = (toward, packs, away)[offset // 3]
        slot = offset % 3 if out is packs else 17 * (offset % 3) + 16
        out[slot] = pack_virtual(offset, vcounts, vdata, vcells, lines)
    high, low = high_low(grid[16, 0:32, :])
    away[51] = high
    away[52] = low
    high, low = high_low(
        jnp.concatenate([grid[16, 32:40, :], jnp.zeros((8, 128), F32)], 0)
    )
    away[53] = jnp.concatenate([high, low], 0)
    deposit_ghosts(
        OUTER,
        FIRST_UNROLLS,
        counts,
        lambda group, chunk: data[group, chunk],
        lambda group, at: cells[pl.ds(group, 1), pl.ds(at, LANES)],
        (toward, away),
        total,
        fields,
        places,
        number,
        copies[4:],
    )


def first_part(counts, vcounts, tcounts, data, cells, vdata, vcells, tdata, tcells):
    slots = cells.shape[3]
    patches = 16 * len(OUTER)
    full = pl.BlockSpec(memory_space=pltpu.VMEM)
    smem = pl.BlockSpec(memory_space=pltpu.SMEM)
    hbm = pl.BlockSpec(memory_space=pltpu.HBM)
    return pl.pallas_call(
        first_kernel,
        in_specs=[smem] * 3 + [hbm] * 6,
        out_specs=[full] * 5,
        scratch_shapes=[
            pltpu.VMEM((patches, slots // LANES, 8, 128), BF16),
            pltpu.VMEM((patches, slots), I32),
            pltpu.VMEM(vdata.shape, BF16),
            pltpu.VMEM(vcells.shape, I32),
            pltpu.VMEM(tdata.shape, BF16),
            pltpu.VMEM(tcells.shape, I32),
            pltpu.VMEM((17, 40, 128), F32),
            pltpu.VMEM((8, 48, 128), F32),
            pltpu.VMEM((8, 8, 128), F32),
            pltpu.VMEM((144, 256), F32),
            pltpu.VMEM((patches, 64, 128), F32),
            pltpu.VMEM((max(FIRST_UNROLLS), 32, 128), F32),
            pltpu.VMEM((max(FIRST_UNROLLS), 8, LANES), F32),
            pltpu.VMEM((32, 128), F32),
            pltpu.SMEM((patches + EXTRA,), I32),
            pltpu.SemaphoreType.DMA((16,)),
        ],
        out_shape=[
            jax.ShapeDtypeStruct((51, 32, 128), BF16),
            jax.ShapeDtypeStruct((54, 32, 128), BF16),
            jax.ShapeDtypeStruct((3, 32, 128), BF16),
            jax.ShapeDtypeStruct((16, 32, 128), F32),
            jax.ShapeDtypeStruct((16, 128), F32),
        ],
        compiler_params=pltpu.CompilerParams(vmem_limit_bytes=FIRST_LIMIT),
        cost_estimate=pl.CostEstimate(
            flops=4 * patches * slots * 64 * 128, bytes_accessed=4000000, transcendentals=0
        ),
        name="first",
    )(counts, vcounts, tcounts, data, cells, vdata, vcells, tdata, tcells)


def own_kernel(
    offsets, counts, data, cells, *rest
):
    out, total, fields, places, number = rest[-5:]

    def split(group):
        return offsets[0] + 2 * (group >> 4), group & 15

    def get_data(group, chunk):
        offset, patch = split(group)
        return data[offset, patch, chunk]

    def get_cells(group, at):
        offset, patch = split(group)
        return cells[0, offset, pl.ds(patch, 1), pl.ds(at, LANES)]

    total[...] = jnp.zeros_like(total)
    deposit_ghosts(
        offsets, OWN_UNROLLS, counts, get_data, get_cells, (out,), total, fields, places, number, ()
    )


def own_part(offsets, counts, data, cells, wait):
    slots = cells.shape[3]
    waits = () if wait is None else (wait,)
    patches = 16 * len(offsets)
    full = pl.BlockSpec(memory_space=pltpu.VMEM)
    smem = pl.BlockSpec(memory_space=pltpu.SMEM)
    anywhere = pl.BlockSpec(memory_space=pl.ANY)
    return pl.pallas_call(
        functools.partial(own_kernel, offsets),
        in_specs=[smem, full, full] + [anywhere] * len(waits),
        out_specs=full,
        scratch_shapes=[
            pltpu.VMEM((patches, 64, 128), F32),
            pltpu.VMEM((max(OWN_UNROLLS), 32, 128), F32),
            pltpu.VMEM((max(OWN_UNROLLS), 8, LANES), F32),
            pltpu.SMEM((patches + EXTRA,), I32),
        ],
        out_shape=jax.ShapeDtypeStruct((patches, 32, 128), BF16),
        compiler_params=pltpu.CompilerParams(vmem_limit_bytes=VMEM_LIMIT),
        cost_estimate=pl.CostEstimate(
            flops=4 * patches * slots * 64 * 128, bytes_accessed=4000000, transcendentals=0
        ),
        name="own",
    )(counts, data, cells, *waits)


def virtual_deposit(packs, out, lines, fields):
    lanes = 512
    rows = sublane(16, lanes)
    zero = jnp.zeros((16, lanes), BF16)

    def place(at):
        return (rows + float(at)).astype(BF16)

    for which, (source, slot) in enumerate(packs):
        f = fields.at[which & 1]
        g = lines.at[which & 1]
        g[...] = source[slot].astype(F32)

        def value(field):
            return jnp.concatenate(
                [g[4 * field + quarter : 4 * field + quarter + 1, :] for quarter in range(4)], 1
            )

        cell = (value(4) * 256.0 + value(5)).astype(I32)
        mass, fx, fy, fz = value(0), value(1), value(2), value(3)
        f[0:1, :] = fx
        f[1:2, :] = 1.0 - fx
        f[2:3, :] = fy
        f[3:4, :] = 1.0 - fy
        f[4:5, :] = fz * mass
        f[5:6, :] = (1.0 - fz) * mass
        f[10:11, :] = (cell >> 12).astype(F32)
        f[11:12, :] = ((cell >> 7) & 31).astype(F32)
        f[12:13, :] = (cell & 127).astype(F32)
        f[13:14, :] = ((cell + 1) & 127).astype(F32)
        x = jnp.concatenate([row8(f, 10)] * 2, 0)
        low_x = jnp.concatenate([row8(f, 1)] * 2, 0)
        high_x = jnp.concatenate([row8(f, 0)] * 2, 0)
        f[16:32, :] = jnp.where(
            rows == x, low_x, jnp.where(rows - 1.0 == x, high_x, 0.0)
        )
        y, z, z_next = row16(f, 11), row16(f, 12), row16(f, 13)
        c0, c1 = row16(f, 5), row16(f, 4)
        y0, y1 = row16(f, 3), row16(f, 2)
        along_y = [
            jnp.where(place(16 * h) == y, y0, jnp.where(place(16 * h - 1) == y, y1, zero))
            for h in range(2)
        ]
        along_z = jnp.concatenate(
            [
                jnp.where(
                    place(16 * k) == z, c0, jnp.where(place(16 * k) == z_next, c1, zero)
                )
                for k in range(8)
            ],
            0,
        )
        left = []
        for k in range(16):
            w = row16(f, 16 + k)
            left += [w * along_y[0], w * along_y[1]]
        out[...] += dot_nt(jnp.concatenate(left, 0), along_z)


def base_kernel(
    tcounts, tdata, tcells, packs, right, left, core, out, lines, fields, grid, tile_fields,
    tile_places, depth
):
    grid[...] = jnp.zeros_like(grid)
    grid[0:16, 0:32, :] = core[...]
    deposit_tiles((0, 3), tcounts, tdata, tcells, grid, tile_fields, tile_places, depth)
    out[...] = grid[0:16, 0:32, :].reshape(512, 128)
    out[0:32, :] += left[51].astype(F32) + left[52].astype(F32)
    virtual_deposit([(packs, 1), (right, 33), (left, 33)], out, lines, fields)


def base_part(*args):
    full = pl.BlockSpec(memory_space=pltpu.VMEM)
    smem = pl.BlockSpec(memory_space=pltpu.SMEM)
    return pl.pallas_call(
        base_kernel,
        in_specs=[smem] + [full] * 6,
        out_specs=full,
        out_shape=jax.ShapeDtypeStruct((512, 128), F32),
        scratch_shapes=[
            pltpu.VMEM((2, 32, 128), F32),
            pltpu.VMEM((2, 32, 512), F32),
            pltpu.VMEM((17, 40, 128), F32),
            pltpu.VMEM((8, 48, 128), F32),
            pltpu.VMEM((8, 8, 128), F32),
            pltpu.VMEM((144, 256), F32),
        ],
        compiler_params=pltpu.CompilerParams(vmem_limit_bytes=VMEM_LIMIT),
        cost_estimate=pl.CostEstimate(
            flops=6 * 3 * 512 * 512 * 128, bytes_accessed=1000000, transcendentals=0
        ),
        name="base",
    )(*args)


def join_kernel(own, packs, right, left, face_y, up, down):
    for at, (out, slot) in enumerate(((up, 0), (down, 34))):
        for patch in range(16):
            out[patch] = (
                own[16 * at + patch].astype(F32)
                + right[slot + patch].astype(F32)
                + left[slot + patch].astype(F32)
            ).astype(BF16)
        out[16] = packs[2 * at]
        out[17] = right[slot + 16]
        out[18] = left[slot + 16]
    corner = left[53].astype(F32)
    row = lax.broadcasted_iota(I32, (16, 128), 0)
    face = face_y[...] + jnp.where(row == 0, corner[0:16] + corner[16:32], 0.0)
    high, low = high_low(face)
    down[19] = jnp.concatenate([high, low], 0)


def join_part(*args):
    full = pl.BlockSpec(memory_space=pltpu.VMEM)
    return pl.pallas_call(
        join_kernel,
        in_specs=[full] * 5,
        out_specs=[full] * 2,
        out_shape=[jax.ShapeDtypeStruct((size, 32, 128), BF16) for size in (19, 20)],
        compiler_params=pltpu.CompilerParams(vmem_limit_bytes=VMEM_LIMIT),
        name="join",
    )(*args)


def last_kernel(
    part, own, right, left, up, down, base_hbm, out_hbm, patches, fields, lines, base, out, sems
):
    for patch in range(16):
        mass = (
            (own[patch].astype(F32) + left[17 + patch].astype(F32))
            + (right[17 + patch].astype(F32) + up[patch].astype(F32))
        ) + down[patch].astype(F32)
        patches[32 * patch : 32 * patch + 32, :] = mass
    for group in range(2):
        for half in range(2):
            for x in range(16):
                block = patches[pl.ds(256 * group + 16 * half + x, 8, stride=32), :]
                at = 128 * (2 * x + half)
                out[8 * group : 8 * group + 8, at : at + 128] = block
    fine_copy = pltpu.make_async_copy(out, out_hbm, sems.at[0])
    fine_copy.start()
    base[...] = part[...]
    both = down[19].astype(F32)
    face = both[0:16] + both[16:32]
    for x in range(16):
        base[32 * x : 32 * x + 1, :] += face[x : x + 1, :]
    virtual_deposit(
        [(source, slot) for source in (up, down) for slot in (16, 17, 18)], base, lines, fields
    )
    base_copy = pltpu.make_async_copy(base, base_hbm, sems.at[1])
    base_copy.start()
    fine_copy.wait()
    base_copy.wait()


def last_part(*args):
    full = pl.BlockSpec(memory_space=pltpu.VMEM)
    return pl.pallas_call(
        last_kernel,
        in_specs=[full] * 6,
        out_specs=[pl.BlockSpec(memory_space=pl.ANY)] * 2,
        out_shape=[
            jax.ShapeDtypeStruct((512, 128), F32),
            jax.ShapeDtypeStruct((16, 4096), F32),
        ],
        scratch_shapes=[
            pltpu.VMEM((512, 128), F32),
            pltpu.VMEM((2, 32, 512), F32),
            pltpu.VMEM((2, 32, 128), F32),
            pltpu.VMEM((512, 128), F32),
            pltpu.VMEM((16, 4096), F32),
            pltpu.SemaphoreType.DMA((2,)),
        ],
        compiler_params=pltpu.CompilerParams(vmem_limit_bytes=VMEM_LIMIT),
        name="last",
    )(*args)


def on_device(
    part_data,
    tile_cells,
    tile_counts,
    ghost_data,
    halo_refined_cells,
    ghost_counts,
    virt_data,
    virt_cells,
    phantom_slot_counts,
):
    sources, own_patches, fields, slots = ghost_data.shape[1:]
    tiled = ghost_data.reshape(sources, own_patches, fields, slots // LANES, 2, 128)
    tiled = tiled.transpose(0, 1, 3, 4, 2, 5)
    tiled = tiled.reshape(sources, own_patches, slots // LANES, 8, 128)
    counts = jnp.swapaxes(ghost_counts, 0, 1)
    tiles = part_data.shape
    pairs = part_data.reshape(tiles[0], tiles[1], tiles[2] // 2, 8, tiles[4])
    toward, away, packs, core, face_y = first_part(
        counts,
        phantom_slot_counts,
        tile_counts,
        tiled,
        halo_refined_cells,
        virt_data,
        jnp.swapaxes(virt_cells, 0, 1),
        pairs,
        tile_cells,
    )
    right = shift(toward, "gx", -1)
    left = shift(away, "gx", 1)
    sides = own_part((3, 5), counts, tiled, halo_refined_cells, None)
    up, down = join_part(sides, packs, right, left, face_y)
    from_up = shift(up, "gy", -1)
    from_down = shift(down, "gy", 1)
    own = own_part((4,), counts, tiled, halo_refined_cells, down)
    part = base_part(tile_counts, pairs, tile_cells, packs, right, left, core)
    base, fine_mass = last_part(part, own, right, left, from_up, from_down)
    return base.reshape(16, 32, 128), fine_mass


def solution(mesh):
    return jax.shard_map(
        on_device,
        mesh=mesh,
        in_specs=(
            P("gx", "gy", None, None, None),
            P("gx", "gy", None, None),
            P("gx", "gy", None),
            P(("gx", "gy"), None, None, None, None),
            P(("gx", "gy"), None, None, None),
            P(("gx", "gy"), None, None),
            P(("gx", "gy"), None, None, None),
            P(("gx", "gy"), None, None),
            P(("gx", "gy"), None),
        ),
        out_specs=(P("gx", "gy", None), P(("gx", "gy"), None)),
        check_vma=False,
    )
```

```python
import functools

import jax
import jax.numpy as jnp
from jax import lax
from jax.experimental import pallas as pl
from jax.experimental.pallas import tpu as pltpu
from jax.sharding import PartitionSpec as P

BF16 = jnp.bfloat16
F32 = jnp.float32
I32 = jnp.int32
NT = (((1,), (1,)), ((), ()))
LANES = 256
FIRST_UNROLLS = (48, 16)
OWN_UNROLLS = (48, 16)
EXTRA = 24
OUTER = (0, 1, 2, 6, 7, 8)
VMEM_LIMIT = 16 * 2**20
FIRST_LIMIT = 56 * 2**20


def shift(x, axis, by):
    devices = lax.axis_size(axis)
    return lax.ppermute(x, axis, [(i, (i + by) % devices) for i in range(devices)])


def sublane(rows, lanes):
    return lax.broadcasted_iota(I32, (rows, lanes), 0).astype(F32)


def dot_nt(a, b):
    return lax.dot_general(a, b, NT, preferred_element_type=F32)


def row8(ref, row):
    return ref[pl.ds(row, 8, stride=0), :]


def row16(ref, row):
    return jnp.concatenate([row8(ref, row)] * 2, 0).astype(BF16)


def high_low(x):
    high = x.astype(BF16)
    return high, (x - high.astype(F32)).astype(BF16)


def pack_virtual(offset, counts, data, cells, lines):
    lane = lax.broadcasted_iota(I32, (1, 512), 1)
    high = data[0, offset].astype(F32)
    cell = cells[offset]
    values = [
        jnp.where(lane < counts[0, offset], high[0:1], 0.0),
        high[1:2],
        high[2:3],
        high[3:4],
        (cell >> 8).astype(F32),
        (cell & 255).astype(F32),
    ]
    for field, value in enumerate(values):
        for quarter in range(4):
            at = 4 * field + quarter
            lines[at : at + 1, :] = value[:, 128 * quarter : 128 * quarter + 128]
    lines[24:32, :] = jnp.zeros((8, 128), F32)
    return lines[...].astype(BF16)


def deposit_ghosts(offsets, unrolls, counts, get_data, get_cells, outs, total, fields, places, number, ready):
    split = len(outs)
    patches = 16 * len(offsets)
    each = len(offsets) // split
    work = jnp.int32(0)
    for at, offset in enumerate(offsets):
        for patch in range(16):
            live = counts[offset, 0, patch]
            number[16 * at + patch] = live
            work = work + jnp.maximum((live + (LANES - 1)) >> 8, 1)
    for extra in range(EXTRA):
        number[patches + extra] = 0
    lane = lax.broadcasted_iota(I32, (8, 128), 1)
    here = sublane(16, 128).astype(BF16)
    before = (sublane(16, 128) - 1.0).astype(BF16)
    rows = sublane(8, 128)
    zero = jnp.zeros((16, 128), BF16)
    for copy in ready:
        copy.wait()

    def deposit(unit, group, start, live, next_one, next_two):
        patch = jnp.minimum(group, patches - 1)
        at = pl.multiple_of(start, LANES)
        high = get_data(patch, start >> 8).astype(F32)
        cell = get_cells(patch, at)
        f = fields.at[unit]
        g = places.at[unit]
        f[0:8, :] = high
        f[8:16, :] = 1.0 - high
        g[0:1, :] = (cell >> 8).astype(F32)
        g[1:2, :] = (cell & 15).astype(F32)
        g[2:3, :] = ((cell >> 4) & 3).astype(F32)
        g[3:4, :] = ((cell >> 6) & 3).astype(F32)
        left, right = [], []
        for half in range(2):
            wide = slice(128 * half, 128 * half + 128)

            def up(field, half=half):
                return row8(f, 4 * half + field)

            def down(field, half=half):
                return row8(f, 8 + 4 * half + field)

            def double(x):
                return jnp.concatenate([x, x], 0).astype(BF16)

            def where_at(field, wide=wide):
                return g[pl.ds(field, 8, stride=0), :][:, wide]

            mass = jnp.where(lane < live - 128 * half, up(0), 0.0)
            c0, c1 = double(down(3) * mass), double(up(3) * mass)
            x0, x1 = double(down(1)), double(up(1))
            inner = where_at(2)
            f[16 + 8 * half : 24 + 8 * half, :] = jnp.where(
                rows == inner, down(2), jnp.where(rows - 1.0 == inner, up(2), 0.0)
            )
            x, z, outer = double(where_at(0)), double(where_at(1)), double(where_at(3))
            along_x = jnp.where(here == x, x0, jnp.where(before == x, x1, zero))
            along_z = jnp.where(here == z, c0, jnp.where(before == z, c1, zero))
            left.append(
                jnp.concatenate(
                    [jnp.where(outer == BF16(k), along_x, zero) for k in range(4)], 0
                )
            )
            right.append(
                jnp.concatenate(
                    [row16(f, 16 + 8 * half + k) * along_z for k in range(5)], 0
                )
            )
        total[patch, :, 0:80] += dot_nt(
            jnp.concatenate(left, 1), jnp.concatenate(right, 1)
        )
        last = live <= LANES
        group = jnp.where(last, group + 1, group)
        return (
            group,
            jnp.where(last, 0, start + LANES),
            jnp.where(last, next_one, live - LANES),
            jnp.where(last, next_two, next_one),
            number[group + 2],
        )

    none = jnp.int32(0)
    state = (none, none, number[0], number[1], number[2])
    for unroll in unrolls:
        if unroll == unrolls[-1]:
            steps = lax.div(work + (unroll - 1), unroll)
        else:
            steps = lax.div(work, unroll)
            work = work - steps * unroll

        def body(_, state, unroll=unroll):
            for unit in range(unroll):
                state = deposit(unit, *state)
            return state

        state = lax.fori_loop(0, steps, body, state)
    lane = lax.broadcasted_iota(I32, (16, 128), 1)

    for index in range(split):
        out = outs[index]

        def fold(k, _, index=index, out=out):
            group = 16 * each * index + k
            for half in range(2):
                at = 32 * half
                even = total[group, at : at + 16]
                odd = total[group, at + 16 : at + 32]
                prior = total[group, at - 16 : at] if half else jnp.zeros((16, 128), F32)
                swapped = pltpu.roll(jnp.where(lane < 64, odd, prior), 64, 1)
                out[k + (k >> 4) if split > 1 else k, 16 * half : 16 * half + 16] = (even + swapped).astype(BF16)
            return 0

        lax.fori_loop(0, 16 * each, fold, 0, unroll=16)


def deposit_tiles(columns, counts, data, cells, grid, fields, places, depth, total=None):
    lane = lax.broadcasted_iota(I32, (8, 128), 1)
    here = sublane(16, 128).astype(BF16)
    before = (sublane(16, 128) - 1.0).astype(BF16)
    fifteen = (sublane(16, 128) + 15.0).astype(BF16)
    rows = sublane(16, 128)
    odd = lax.broadcasted_iota(I32, (2, 128), 0) * 8
    zero = jnp.zeros((16, 128), BF16)

    def double(x):
        return jnp.concatenate([x, x], 0).astype(BF16)

    def column(col, _):
        tx = col >> 2
        ty = col & 3
        depth[...] = jnp.zeros_like(depth)
        if total is not None:
            patches = total.shape[0]
            share = -(-patches // (columns[1] - columns[0]))
            begin = jnp.minimum((col - columns[0]) * share, patches - share)
            total[pl.ds(begin, share)] = jnp.zeros((share,) + total.shape[1:], F32)
        for pair in range(8):
            f = fields.at[pair]
            g = places.at[pair]
            high = data[tx, ty, pair].astype(F32)
            cell = cells[tx, ty, 2 * pair : 2 * pair + 2, :]
            f[0:8, :] = high
            f[8:16, :] = 1.0 - high
            g[0:2, :] = (cell >> 6).astype(F32)
            g[2:4, :] = ((cell >> 3) & 7).astype(F32)
            g[4:6, :] = ((cell & 7) + odd).astype(F32)
            left, right = [], []
            for half in range(2):
                def up(field, half=half):
                    return row8(f, 4 * half + field)

                def down(field, half=half):
                    return row8(f, 8 + 4 * half + field)

                def wide(x):
                    return jnp.concatenate([x, x], 0)

                mass = jnp.where(lane < counts[tx, ty, 2 * pair + half], up(0), 0.0)
                c0, c1 = double(down(3) * mass), double(up(3) * mass)
                x = wide(row8(g, half))
                f[16 + 16 * half : 32 + 16 * half, :] = jnp.where(
                    rows == x, wide(down(1)), jnp.where(rows - 1.0 == x, wide(up(1)), 0.0)
                )
                y, z = double(row8(g, 2 + half)), double(row8(g, 4 + half))
                along_y = jnp.where(
                    here == y, double(down(2)), jnp.where(before == y, double(up(2)), zero)
                )
                left.append(
                    jnp.concatenate(
                        [jnp.where(here == z, c0, jnp.where(before == z, c1, zero)),
                         jnp.where(fifteen == z, c1, zero)], 0
                    )
                )
                right.append(
                    jnp.concatenate(
                        [row16(f, 16 + 16 * half + k) * along_y for k in range(9)], 0
                    )
                )
            depth[16 * pair : 16 * pair + 32, 0:144] += dot_nt(
                jnp.concatenate(left, 1), jnp.concatenate(right, 1)
            )
        depth[0:16, :] += depth[128:144, :]
        first = jnp.transpose(depth[0:128, 0:128])
        final = jnp.transpose(depth[0:128, 128:256])
        at = pl.ds(pl.multiple_of(8 * ty, 8), 16)
        for k in range(8):
            grid[8 * tx + k, at, :] += first[16 * k : 16 * k + 16]
        grid[8 * tx + 8, at, :] += final[0:16]
        return 0

    lax.fori_loop(*columns, column, 0)


def first_kernel(
    counts, vcounts, tcounts, data_hbm, cells_hbm, vdata_hbm, vcells_hbm, tdata_hbm, tcells_hbm,
    toward, away, packs, core, face_y,
    data, cells, vdata, vcells, tdata, tcells, grid, tile_fields, tile_places, depth, total, fields, places, lines, number, sems,
):
    sources = [(tdata_hbm, tdata), (tcells_hbm, tcells), (vdata_hbm, vdata), (vcells_hbm, vcells)]
    for at, offset in enumerate(OUTER):
        here = pl.ds(16 * at, 16)
        sources.append((data_hbm.at[offset], data.at[here]))
        sources.append((cells_hbm.at[0, offset], cells.at[here]))
    copies = [
        pltpu.make_async_copy(source, target, sems.at[index])
        for index, (source, target) in enumerate(sources)
    ]
    for copy in copies:
        copy.start()
    grid[...] = jnp.zeros_like(grid)
    for copy in copies[:2]:
        copy.wait()
    deposit_tiles((3, 8), tcounts, tdata, tcells, grid, tile_fields, tile_places, depth, total)
    core[...] = grid[0:16, 0:32, :]
    face_y[...] = grid[0:16, 32, :]
    for copy in copies[2:4]:
        copy.wait()
    for offset in range(9):
        out = (toward, packs, away)[offset // 3]
        slot = offset % 3 if out is packs else 17 * (offset % 3) + 16
        out[slot] = pack_virtual(offset, vcounts, vdata, vcells, lines)
    high, low = high_low(grid[16, 0:32, :])
    away[51] = high
    away[52] = low
    high, low = high_low(
        jnp.concatenate([grid[16, 32:40, :], jnp.zeros((8, 128), F32)], 0)
    )
    away[53] = jnp.concatenate([high, low], 0)
    deposit_ghosts(
        OUTER,
        FIRST_UNROLLS,
        counts,
        lambda group, chunk: data[group, chunk],
        lambda group, at: cells[pl.ds(group, 1), pl.ds(at, LANES)],
        (toward, away),
        total,
        fields,
        places,
        number,
        copies[4:],
    )


def first_part(counts, vcounts, tcounts, data, cells, vdata, vcells, tdata, tcells):
    slots = cells.shape[3]
    patches = 16 * len(OUTER)
    full = pl.BlockSpec(memory_space=pltpu.VMEM)
    smem = pl.BlockSpec(memory_space=pltpu.SMEM)
    hbm = pl.BlockSpec(memory_space=pltpu.HBM)
    return pl.pallas_call(
        first_kernel,
        in_specs=[smem] * 3 + [hbm] * 6,
        out_specs=[full] * 5,
        scratch_shapes=[
            pltpu.VMEM((patches, slots // LANES, 8, 128), BF16),
            pltpu.VMEM((patches, slots), I32),
            pltpu.VMEM(vdata.shape, BF16),
            pltpu.VMEM(vcells.shape, I32),
            pltpu.VMEM(tdata.shape, BF16),
            pltpu.VMEM(tcells.shape, I32),
            pltpu.VMEM((17, 40, 128), F32),
            pltpu.VMEM((8, 56, 128), F32),
            pltpu.VMEM((8, 16, 128), F32),
            pltpu.VMEM((144, 256), F32),
            pltpu.VMEM((patches, 64, 128), F32),
            pltpu.VMEM((max(FIRST_UNROLLS), 40, 128), F32),
            pltpu.VMEM((max(FIRST_UNROLLS), 16, LANES), F32),
            pltpu.VMEM((32, 128), F32),
            pltpu.SMEM((patches + EXTRA,), I32),
            pltpu.SemaphoreType.DMA((16,)),
        ],
        out_shape=[
            jax.ShapeDtypeStruct((51, 32, 128), BF16),
            jax.ShapeDtypeStruct((54, 32, 128), BF16),
            jax.ShapeDtypeStruct((3, 32, 128), BF16),
            jax.ShapeDtypeStruct((16, 32, 128), F32),
            jax.ShapeDtypeStruct((16, 128), F32),
        ],
        compiler_params=pltpu.CompilerParams(vmem_limit_bytes=FIRST_LIMIT),
        cost_estimate=pl.CostEstimate(
            flops=4 * patches * slots * 64 * 128, bytes_accessed=4000000, transcendentals=0
        ),
        name="first",
    )(counts, vcounts, tcounts, data, cells, vdata, vcells, tdata, tcells)


def own_kernel(
    offsets, counts, data, cells, *rest
):
    out, total, fields, places, number = rest[-5:]

    def split(group):
        return offsets[0] + 2 * (group >> 4), group & 15

    def get_data(group, chunk):
        offset, patch = split(group)
        return data[offset, patch, chunk]

    def get_cells(group, at):
        offset, patch = split(group)
        return cells[0, offset, pl.ds(patch, 1), pl.ds(at, LANES)]

    total[...] = jnp.zeros_like(total)
    deposit_ghosts(
        offsets, OWN_UNROLLS, counts, get_data, get_cells, (out,), total, fields, places, number, ()
    )


def own_part(offsets, counts, data, cells, wait):
    slots = cells.shape[3]
    waits = () if wait is None else (wait,)
    patches = 16 * len(offsets)
    full = pl.BlockSpec(memory_space=pltpu.VMEM)
    smem = pl.BlockSpec(memory_space=pltpu.SMEM)
    anywhere = pl.BlockSpec(memory_space=pl.ANY)
    return pl.pallas_call(
        functools.partial(own_kernel, offsets),
        in_specs=[smem, full, full] + [anywhere] * len(waits),
        out_specs=full,
        scratch_shapes=[
            pltpu.VMEM((patches, 64, 128), F32),
            pltpu.VMEM((max(OWN_UNROLLS), 40, 128), F32),
            pltpu.VMEM((max(OWN_UNROLLS), 16, LANES), F32),
            pltpu.SMEM((patches + EXTRA,), I32),
        ],
        out_shape=jax.ShapeDtypeStruct((patches, 32, 128), BF16),
        compiler_params=pltpu.CompilerParams(vmem_limit_bytes=VMEM_LIMIT),
        cost_estimate=pl.CostEstimate(
            flops=4 * patches * slots * 64 * 128, bytes_accessed=4000000, transcendentals=0
        ),
        name="own",
    )(counts, data, cells, *waits)


def virtual_deposit(packs, out, lines, fields):
    lanes = 512
    rows = sublane(16, lanes)
    zero = jnp.zeros((16, lanes), BF16)

    def place(at):
        return (rows + float(at)).astype(BF16)

    for which, (source, slot) in enumerate(packs):
        f = fields.at[which & 1]
        g = lines.at[which & 1]
        g[...] = source[slot].astype(F32)

        def value(field):
            return jnp.concatenate(
                [g[4 * field + quarter : 4 * field + quarter + 1, :] for quarter in range(4)], 1
            )

        cell = (value(4) * 256.0 + value(5)).astype(I32)
        mass, fx, fy, fz = value(0), value(1), value(2), value(3)
        f[0:1, :] = fx
        f[1:2, :] = 1.0 - fx
        f[2:3, :] = fy
        f[3:4, :] = 1.0 - fy
        f[4:5, :] = fz * mass
        f[5:6, :] = (1.0 - fz) * mass
        f[10:11, :] = (cell >> 12).astype(F32)
        f[11:12, :] = ((cell >> 7) & 31).astype(F32)
        f[12:13, :] = (cell & 127).astype(F32)
        f[13:14, :] = ((cell + 1) & 127).astype(F32)
        x = jnp.concatenate([row8(f, 10)] * 2, 0)
        low_x = jnp.concatenate([row8(f, 1)] * 2, 0)
        high_x = jnp.concatenate([row8(f, 0)] * 2, 0)
        f[16:32, :] = jnp.where(
            rows == x, low_x, jnp.where(rows - 1.0 == x, high_x, 0.0)
        )
        y, z, z_next = row16(f, 11), row16(f, 12), row16(f, 13)
        c0, c1 = row16(f, 5), row16(f, 4)
        y0, y1 = row16(f, 3), row16(f, 2)
        along_y = [
            jnp.where(place(16 * h) == y, y0, jnp.where(place(16 * h - 1) == y, y1, zero))
            for h in range(2)
        ]
        along_z = jnp.concatenate(
            [
                jnp.where(
                    place(16 * k) == z, c0, jnp.where(place(16 * k) == z_next, c1, zero)
                )
                for k in range(8)
            ],
            0,
        )
        left = []
        for k in range(16):
            w = row16(f, 16 + k)
            left += [w * along_y[0], w * along_y[1]]
        out[...] += dot_nt(jnp.concatenate(left, 0), along_z)


def base_kernel(
    tcounts, tdata, tcells, packs, right, left, core, out, lines, fields, grid, tile_fields,
    tile_places, depth
):
    grid[...] = jnp.zeros_like(grid)
    grid[0:16, 0:32, :] = core[...]
    deposit_tiles((0, 3), tcounts, tdata, tcells, grid, tile_fields, tile_places, depth)
    out[...] = grid[0:16, 0:32, :].reshape(512, 128)
    out[0:32, :] += left[51].astype(F32) + left[52].astype(F32)
    virtual_deposit([(packs, 1), (right, 33), (left, 33)], out, lines, fields)


def base_part(*args):
    full = pl.BlockSpec(memory_space=pltpu.VMEM)
    smem = pl.BlockSpec(memory_space=pltpu.SMEM)
    return pl.pallas_call(
        base_kernel,
        in_specs=[smem] + [full] * 6,
        out_specs=full,
        out_shape=jax.ShapeDtypeStruct((512, 128), F32),
        scratch_shapes=[
            pltpu.VMEM((2, 32, 128), F32),
            pltpu.VMEM((2, 40, 512), F32),
            pltpu.VMEM((17, 40, 128), F32),
            pltpu.VMEM((8, 56, 128), F32),
            pltpu.VMEM((8, 16, 128), F32),
            pltpu.VMEM((144, 256), F32),
        ],
        compiler_params=pltpu.CompilerParams(vmem_limit_bytes=VMEM_LIMIT),
        cost_estimate=pl.CostEstimate(
            flops=6 * 3 * 512 * 512 * 128, bytes_accessed=1000000, transcendentals=0
        ),
        name="base",
    )(*args)


def join_kernel(own, packs, right, left, face_y, up, down):
    for at, (out, slot) in enumerate(((up, 0), (down, 34))):
        for patch in range(16):
            out[patch] = (
                own[16 * at + patch].astype(F32)
                + right[slot + patch].astype(F32)
                + left[slot + patch].astype(F32)
            ).astype(BF16)
        out[16] = packs[2 * at]
        out[17] = right[slot + 16]
        out[18] = left[slot + 16]
    corner = left[53].astype(F32)
    row = lax.broadcasted_iota(I32, (16, 128), 0)
    face = face_y[...] + jnp.where(row == 0, corner[0:16] + corner[16:32], 0.0)
    high, low = high_low(face)
    down[19] = jnp.concatenate([high, low], 0)


def join_part(*args):
    full = pl.BlockSpec(memory_space=pltpu.VMEM)
    return pl.pallas_call(
        join_kernel,
        in_specs=[full] * 5,
        out_specs=[full] * 2,
        out_shape=[jax.ShapeDtypeStruct((size, 32, 128), BF16) for size in (19, 20)],
        compiler_params=pltpu.CompilerParams(vmem_limit_bytes=VMEM_LIMIT),
        name="join",
    )(*args)


def last_kernel(
    part, own, right, left, up, down, base_hbm, out_hbm, patches, fields, lines, base, out, sems
):
    for patch in range(16):
        mass = (
            (own[patch].astype(F32) + left[17 + patch].astype(F32))
            + (right[17 + patch].astype(F32) + up[patch].astype(F32))
        ) + down[patch].astype(F32)
        patches[32 * patch : 32 * patch + 32, :] = mass
    for group in range(2):
        for half in range(2):
            for x in range(16):
                block = patches[pl.ds(256 * group + 16 * half + x, 8, stride=32), :]
                at = 128 * (2 * x + half)
                out[8 * group : 8 * group + 8, at : at + 128] = block
    fine_copy = pltpu.make_async_copy(out, out_hbm, sems.at[0])
    fine_copy.start()
    base[...] = part[...]
    both = down[19].astype(F32)
    face = both[0:16] + both[16:32]
    for x in range(16):
        base[32 * x : 32 * x + 1, :] += face[x : x + 1, :]
    virtual_deposit(
        [(source, slot) for source in (up, down) for slot in (16, 17, 18)], base, lines, fields
    )
    base_copy = pltpu.make_async_copy(base, base_hbm, sems.at[1])
    base_copy.start()
    fine_copy.wait()
    base_copy.wait()


def last_part(*args):
    full = pl.BlockSpec(memory_space=pltpu.VMEM)
    return pl.pallas_call(
        last_kernel,
        in_specs=[full] * 6,
        out_specs=[pl.BlockSpec(memory_space=pl.ANY)] * 2,
        out_shape=[
            jax.ShapeDtypeStruct((512, 128), F32),
            jax.ShapeDtypeStruct((16, 4096), F32),
        ],
        scratch_shapes=[
            pltpu.VMEM((512, 128), F32),
            pltpu.VMEM((2, 40, 512), F32),
            pltpu.VMEM((2, 32, 128), F32),
            pltpu.VMEM((512, 128), F32),
            pltpu.VMEM((16, 4096), F32),
            pltpu.SemaphoreType.DMA((2,)),
        ],
        compiler_params=pltpu.CompilerParams(vmem_limit_bytes=VMEM_LIMIT),
        name="last",
    )(*args)


def on_device(
    part_data,
    tile_cells,
    tile_counts,
    ghost_data,
    halo_refined_cells,
    ghost_counts,
    virt_data,
    virt_cells,
    phantom_slot_counts,
):
    sources, own_patches, fields, slots = ghost_data.shape[1:]
    tiled = ghost_data.reshape(sources, own_patches, fields, slots // LANES, 2, 128)
    tiled = tiled.transpose(0, 1, 3, 4, 2, 5)
    tiled = tiled.reshape(sources, own_patches, slots // LANES, 8, 128)
    counts = jnp.swapaxes(ghost_counts, 0, 1)
    tiles = part_data.shape
    pairs = part_data.reshape(tiles[0], tiles[1], tiles[2] // 2, 8, tiles[4])
    toward, away, packs, core, face_y = first_part(
        counts,
        phantom_slot_counts,
        tile_counts,
        tiled,
        halo_refined_cells,
        virt_data,
        jnp.swapaxes(virt_cells, 0, 1),
        pairs,
        tile_cells,
    )
    right = shift(toward, "gx", -1)
    left = shift(away, "gx", 1)
    sides = own_part((3, 5), counts, tiled, halo_refined_cells, None)
    up, down = join_part(sides, packs, right, left, face_y)
    from_up = shift(up, "gy", -1)
    from_down = shift(down, "gy", 1)
    own = own_part((4,), counts, tiled, halo_refined_cells, down)
    part = base_part(tile_counts, pairs, tile_cells, packs, right, left, core)
    base, fine_mass = last_part(part, own, right, left, from_up, from_down)
    return base.reshape(16, 32, 128), fine_mass


def solution(mesh):
    return jax.shard_map(
        on_device,
        mesh=mesh,
        in_specs=(
            P("gx", "gy", None, None, None),
            P("gx", "gy", None, None),
            P("gx", "gy", None),
            P(("gx", "gy"), None, None, None, None),
            P(("gx", "gy"), None, None, None),
            P(("gx", "gy"), None, None),
            P(("gx", "gy"), None, None, None),
            P(("gx", "gy"), None, None),
            P(("gx", "gy"), None),
        ),
        out_specs=(P("gx", "gy", None), P(("gx", "gy"), None)),
        check_vma=False,
    )
```
